128 devices in a mesh: ctx: 8 (over y_lo, x), tp: 16 (over z, y_hi, core).
Axes of the slice: x: 4, y: 4 (y_hi: 2, y_lo: 2; y = y_hi * 2 + y_lo), z: 4, core: 2. Of those that a mesh axis runs over, the one named last changes fastest.
Arguments:
- stored_pages: bfloat16 [24, 128, 8192], P('ctx', None, 'tp'), may hold values from -6 to 6
- kv_weight: bfloat16 [8192, 2048], P(None, 'tp'), may hold values from -0.0625 to 0.0625
- page_table: int32 [8, 8], replicated, may hold values from 0 to 23, as said below
- page_counts: int32 [8, 8], replicated, may hold values from 0 to 1, as said below
- queries: bfloat16 [2048, 8192], P('ctx', 'tp'), may hold values from -16 to 16
- turn_kv: bfloat16 [2048, 2048], P('ctx', 'tp'), may hold values from -6 to 6
- turn_pos: int32 [2048], replicated, may hold values from 3072 to 6143, as said below
Outputs:
- attended: bfloat16 [2048, 8192], P('ctx', 'tp')
- restored_cache: bfloat16 [8192, 2048], P('ctx', 'tp')
The draws below stay inside these ranges and needn't reach their ends.
Inputs may be any that keep to these rules, and one draw needn't show every extreme that they name: page_table[d, h] is a page of holder h (h * 3 to h * 3 + 2); where page_counts[d, h] is 0 it is h * 3. Every stored page is taken by exactly one context shard. `page_counts`: each holder hands out all its 3 pages, at most one to each context shard; one context shard takes a page from every holder. `turn_pos`: strictly increasing in steps of 1 or 2; turn_pos[0] = 3072 and the last entry is 6143.
All inputs are finite; a program needn't handle non-finite values.
Results may differ from the reference program's by a relative error of at most 0.03.
Values may be sent and summed in bfloat16 or wider, within the bound.
No kernel may reach another device: no remote copies, remote signals or barrier semaphores. Data moves between devices by JAX's collectives and lax.ppermute only.
A program may use at most 192 MiB of HBM per device.

```python
import math
import jax
import jax.numpy as jnp
from jax import lax

D = 8192
HEADS = 64
KV_HEADS = 8
HEAD_DIM = 128
PAGE = 128
HOLD_PG = 3
PAGES = 24
QN = 2048


def page_plan(key):
    holders = PAGES // HOLD_PG
    hot_key, dest_key = jax.random.split(key, 2)
    hottest = jax.random.randint(hot_key, (), 0, holders).astype(jnp.int32)

    def holder_plan(sub_key):
        first_key, second_key = jax.random.split(sub_key)
        others = jax.random.permutation(first_key, holders - 1)[:HOLD_PG - 1].astype(jnp.int32)
        others = others + (others >= hottest).astype(jnp.int32)
        targets = jnp.concatenate([hottest[None], others])
        ordering = jax.random.permutation(second_key, HOLD_PG).astype(jnp.int32)
        return (targets, ordering)
    targets, orderings = jax.vmap(holder_plan)(jax.random.split(dest_key, holders))
    dest_ids = jnp.arange(holders, dtype=jnp.int32)
    holder_ids = jnp.arange(holders, dtype=jnp.int32)
    matched = targets[None, :, :] == dest_ids[:, None, None]
    counts = jnp.sum(matched.astype(jnp.int32), axis=2)
    table = holder_ids[None, :] * HOLD_PG + jnp.sum(jnp.where(matched, orderings[None, :, :], 0), axis=2)
    return (table.astype(jnp.int32), counts.astype(jnp.int32))


def draw_page_table(key, part):
    return page_plan(key)[0]


def draw_page_counts(key, part):
    return page_plan(key)[1]


def draw_turn_pos(key, part):
    key = jax.random.fold_in(key, 3)
    order = jax.random.permutation(key, QN - 1).astype(jnp.int32)
    increments = jnp.where(order < QN // 2, 2, 1).astype(jnp.int32)
    offsets = jnp.concatenate([jnp.zeros((1,), jnp.int32), jnp.cumsum(increments).astype(jnp.int32)])
    positions = PAGES * PAGE + offsets
    return positions.astype(jnp.int32)


def draw_queries(key, part):
    key = jax.random.fold_in(key, 5)
    values = jnp.clip(jax.random.normal(key, (QN, HEADS, HEAD_DIM), jnp.float32), -6.0, 6.0)
    return values.reshape(QN, HEADS * HEAD_DIM).astype(jnp.bfloat16)


def draw_turn_kv(key, part):
    key = jax.random.fold_in(key, 7)
    values = jnp.clip(jax.random.normal(key, (QN, KV_HEADS, 2, HEAD_DIM), jnp.float32), -6.0, 6.0)
    return values.reshape(QN, 2 * KV_HEADS * HEAD_DIM).astype(jnp.bfloat16)


def shard_levels(key, shape, pieces, low, high):
    gain = 1.0
    for dim, blocks in pieces:
        steps = jax.random.uniform(jax.random.fold_in(jax.random.fold_in(key, 6), dim), (blocks,), jnp.float32, low / len(pieces), high / len(pieces))
        gain = gain * jnp.repeat(jnp.exp(steps), shape[dim] // blocks).reshape((-1,) + (1,) * (len(shape) - 1 - dim))
    return gain


def normal_values(key, shape, scale, most, cuts=(), held_as=jnp.bfloat16):
    level = shard_levels(key, shape, cuts, -0.22, 0.18) if cuts else 1.0
    values = jax.random.normal(key, shape, jnp.float32) * scale * level
    return jnp.minimum(jnp.maximum(values, -most), most).astype(held_as)


def setup_inputs(seed: int = 0) -> dict:
    keys = jax.random.split(jax.random.key(seed), 8)
    return {
        "stored_pages": normal_values(keys[0], (PAGES, PAGE, D), 1.0, 6.0, ((0, 8), (2, 16))),
        "kv_weight": normal_values(keys[1], (D, 2 * KV_HEADS * HEAD_DIM), D ** -0.5, 0.0625, ((1, 16),)),
        "page_table": draw_page_table(jax.random.fold_in(keys[7], 71), 0),
        "page_counts": draw_page_counts(jax.random.fold_in(keys[7], 71), 0),
        "queries": draw_queries(jax.random.fold_in(keys[7], 71), 0),
        "turn_kv": draw_turn_kv(jax.random.fold_in(keys[7], 71), 0),
        "turn_pos": draw_turn_pos(jax.random.fold_in(keys[7], 71), 0),
    }


huge_value = 1e+30
far_position = 1 << 30

def inverse_freq(head_width):
    half_width = head_width // 2
    exponent = jnp.arange(half_width, dtype=jnp.float32) * 2.0 / head_width
    base_freq = jnp.exp(-exponent * math.log(500000.0))
    wavelength = 2.0 * math.pi / base_freq
    smooth = (8192.0 / wavelength - 1.0) / 3.0
    blended = (1.0 - smooth) * base_freq / 8.0 + smooth * base_freq
    return jnp.where(wavelength < 2048.0, base_freq, jnp.where(wavelength > 8192.0, base_freq / 8.0, blended))

def rotate(values, positions):
    head_width = values.shape[-1]
    half_width = head_width // 2
    angle = positions.astype(jnp.float32)[:, None] * inverse_freq(head_width)[None, :]
    angle = angle.reshape((angle.shape[0],) + (1,) * (values.ndim - 2) + (half_width,))
    cosine = jnp.cos(angle)
    sine = jnp.sin(angle)
    first_half = values[..., :half_width]
    second_half = values[..., half_width:]
    return jnp.concatenate([first_half * cosine - second_half * sine, second_half * cosine + first_half * sine], axis=-1)

def rope_blocks(values, positions, first_block):
    row_count = values.shape[0]
    block_count = values.shape[1] // HEAD_DIM
    shaped = values.reshape(row_count, block_count, HEAD_DIM)
    is_key = (first_block + jnp.arange(block_count)) % 2 == 0
    turned = jnp.where(is_key[None, :, None], rotate(shaped, positions), shaped)
    return turned.reshape(row_count, block_count * HEAD_DIM)

def reference(stored_pages, kv_weight, page_table, page_counts, queries, turn_kv, turn_pos):
    row_total = PAGES * PAGE
    projected = jnp.dot(stored_pages.reshape(row_total, D), kv_weight, preferred_element_type=jnp.float32)
    page_keys = rope_blocks(projected, jnp.arange(row_total, dtype=jnp.int32), 0).astype(jnp.bfloat16)
    slot_rows = (page_table.reshape(-1)[:, None] * PAGE + jnp.arange(PAGE, dtype=jnp.int32)[None, :]).reshape(-1).astype(jnp.int32)
    live_rows = jnp.repeat(page_counts.reshape(-1) > 0, PAGE)
    restored_cache = jnp.where(live_rows[:, None], page_keys[slot_rows], jnp.zeros((), jnp.bfloat16))
    turn_keys = rope_blocks(turn_kv.astype(jnp.float32), turn_pos, 0).astype(jnp.bfloat16)
    query_rot = rotate(queries.astype(jnp.float32).reshape(QN, HEADS, HEAD_DIM), turn_pos).astype(jnp.bfloat16)
    every_row = jnp.concatenate([restored_cache, turn_keys], axis=0).reshape(-1, KV_HEADS, 2, HEAD_DIM)
    key_pos = jnp.concatenate([jnp.where(live_rows, -1, far_position).astype(jnp.int32), turn_pos.astype(jnp.int32)])
    key_heads = jnp.transpose(every_row[:, :, 0], (1, 0, 2)).astype(jnp.float32)
    value_heads = jnp.transpose(every_row[:, :, 1], (1, 0, 2))
    visible = key_pos[None, :] <= turn_pos[:, None]
    group_size = HEADS // KV_HEADS
    scale = 1.0 / math.sqrt(HEAD_DIM)

    def one_head(head_index):
        kv_index = head_index // group_size
        query_head = lax.dynamic_index_in_dim(query_rot, head_index, 1, keepdims=False).astype(jnp.float32)
        key_head = lax.dynamic_index_in_dim(key_heads, kv_index, 0, keepdims=False)
        value_head = lax.dynamic_index_in_dim(value_heads, kv_index, 0, keepdims=False)
        scores = jnp.dot(query_head, key_head.T, precision=lax.Precision.HIGHEST) * scale
        largest = lax.optimization_barrier(jnp.max(jnp.where(visible, scores, -huge_value), axis=1))
        weights = jnp.where(visible, jnp.exp(scores - largest[:, None]), 0.0)
        denominator = lax.optimization_barrier(jnp.sum(weights, axis=1))
        rounded_weights = weights.astype(jnp.bfloat16)
        numerator = jnp.dot(rounded_weights, value_head, preferred_element_type=jnp.float32)
        return numerator / denominator[:, None]
    heads_out = lax.map(one_head, jnp.arange(HEADS, dtype=jnp.int32))
    attended = jnp.transpose(heads_out, (1, 0, 2)).reshape(QN, HEADS * HEAD_DIM).astype(jnp.bfloat16)
    return (attended, restored_cache)
```

```python
import functools
import math

import jax
import jax.numpy as jnp
from jax import lax
from jax.experimental import pallas as pl
from jax.experimental.pallas import tpu as pltpu
from jax.sharding import PartitionSpec as P

HEAD_DIM = 128
PAGE = 128
SOURCES = 8
huge_value = 1e30
SCORE_SCALE = math.log2(math.e) / math.sqrt(HEAD_DIM)
VMEM_BYTES = 32 * 1024 * 1024


def swapped(value, bits):
    return lax.ppermute(value, "tp", [(i, i ^ bits) for i in range(lax.axis_size("tp"))])


def inverse_freq(head_width):
    half_width = head_width // 2
    exponent = jnp.arange(half_width, dtype=jnp.float32) * 2.0 / head_width
    base_freq = jnp.exp(-exponent * math.log(500000.0))
    wavelength = 2.0 * math.pi / base_freq
    smooth = (8192.0 / wavelength - 1.0) / 3.0
    blended = (1.0 - smooth) * base_freq / 8.0 + smooth * base_freq
    return jnp.where(
        wavelength < 2048.0, base_freq, jnp.where(wavelength > 8192.0, base_freq / 8.0, blended)
    )


def rope_tables(positions):
    angle = positions.astype(jnp.float32)[:, None] * inverse_freq(HEAD_DIM)[None, :]
    cosine = jnp.cos(angle)
    sine = jnp.sin(angle)
    return (
        jnp.concatenate([cosine, cosine], axis=1),
        jnp.concatenate([-sine, sine], axis=1),
    )


def turned(value, cosine, sine):
    return value * cosine + pltpu.roll(value, HEAD_DIM // 2, 1) * sine


def any_spec():
    return pl.BlockSpec(memory_space=pl.ANY)


def vmem_spec():
    return pl.BlockSpec(memory_space=pltpu.VMEM)


def smem_spec():
    return pl.BlockSpec(memory_space=pltpu.SMEM)


def prepare_kernel(queries, turn_kv, cosine, sine, query_out, turn_out):
    is_key = lax.axis_index("tp") % 2 == 0
    c = cosine[...]
    s = sine[...]
    for head in range(query_out.shape[0]):
        block = queries[:, head * HEAD_DIM : (head + 1) * HEAD_DIM].astype(jnp.float32)
        query_out[head] = turned(block, c, s).astype(jnp.bfloat16)
    block = turn_kv[...].astype(jnp.float32)
    block = turned(block, jnp.where(is_key, c, 1.0), jnp.where(is_key, s, 0.0)).astype(jnp.bfloat16)
    for peer in range(SOURCES):
        turn_out[peer] = block


def project_kernel(x0, x1, x2, x3, weight, w1, w2, w3, own_out, out1, out2, out3, x_buf, w_buf, sems):
    tp = lax.axis_index("tp")
    core = tp % 2
    pair = tp // 8
    spot = (tp // 2) % 4
    depth = x_buf.shape[2]
    copies = []
    for r, x in enumerate((x0, x1, x2, x3)):
        at = spot ^ r
        row = ((pair * 4 + at) * 2 + core) * depth
        group = [pltpu.make_async_copy(x, x_buf.at[r], sems.at[r, 0])]
        group.append(
            pltpu.make_async_copy(
                weight.at[pl.ds(pl.multiple_of(row, depth), depth)],
                w_buf.at[r, :, pl.ds(0, HEAD_DIM)],
                sems.at[r, 1],
            )
        )
        for b, w in enumerate((w1, w2, w3)):
            group.append(
                pltpu.make_async_copy(
                    w.at[at], w_buf.at[r, :, pl.ds((b + 1) * HEAD_DIM, HEAD_DIM)], sems.at[r, b + 2]
                )
            )
        for copy in group:
            copy.start()
        copies.append(group)
    total = None
    for r in range(4):
        for copy in copies[r]:
            copy.wait()
        part = jnp.dot(x_buf[r], w_buf[r], preferred_element_type=jnp.float32)
        total = part if total is None else total + part
    own_out[...] = total[:, :HEAD_DIM]
    for b, out in enumerate((out1, out2, out3)):
        out[...] = total[:, (b + 1) * HEAD_DIM : (b + 2) * HEAD_DIM].astype(jnp.bfloat16)


def finish_kernel(own, p1, p2, p3, cosine, sine, out):
    is_key = lax.axis_index("tp") % 2 == 0
    value = own[...] + p1[...].astype(jnp.float32)
    value = value + (p2[...].astype(jnp.float32) + p3[...].astype(jnp.float32))
    c = jnp.where(is_key, cosine[...], 1.0)
    s = jnp.where(is_key, sine[...], 0.0)
    block = turned(value, c, s).astype(jnp.bfloat16)
    for peer in range(SOURCES):
        out[peer] = block


def scores_of(query, keys):
    return lax.dot_general(
        query, keys, (((1,), (1,)), ((), ())), preferred_element_type=jnp.float32
    )


def softmax_step(state, scores, values):
    top, total, acc = state
    new_top = jnp.maximum(top, jnp.max(scores, axis=1, keepdims=True))
    decay = jnp.exp2((top - new_top) * SCORE_SCALE)
    weights = jnp.exp2((scores - new_top) * SCORE_SCALE)
    total = total * decay + jnp.sum(weights, axis=1, keepdims=True)
    acc = acc * decay + jnp.dot(
        weights.astype(jnp.bfloat16), values, preferred_element_type=jnp.float32
    )
    return new_top, total, acc


def load_pair(own, other, key_buf, value_buf, sems, act):
    core = lax.axis_index("tp") % 2

    @pl.when(core == 0)
    def _():
        act(pltpu.make_async_copy(own, key_buf, sems.at[0]))
        act(pltpu.make_async_copy(other, value_buf, sems.at[1]))

    @pl.when(core == 1)
    def _():
        act(pltpu.make_async_copy(other, key_buf, sems.at[0]))
        act(pltpu.make_async_copy(own, value_buf, sems.at[1]))


def turn_kernel(queries, own, other, top_out, total_out, acc_out, key_buf, value_buf, sems):
    ctx = lax.axis_index("ctx")
    heads, rows, _ = queries.shape
    load_pair(own, other, key_buf, value_buf, sems, lambda copy: copy.start())
    load_pair(own, other, key_buf, value_buf, sems, lambda copy: copy.wait())
    shape = (rows, rows)
    seen = lax.broadcasted_iota(jnp.int32, shape, 1) <= lax.broadcasted_iota(jnp.int32, shape, 0)

    def keep(head, state):
        top, total, acc = state
        top_out[head] = jnp.broadcast_to(top, (rows, HEAD_DIM))
        total_out[head] = jnp.broadcast_to(total, (rows, HEAD_DIM))
        acc_out[head] = acc

    for head in range(heads):
        scores = jnp.where(seen, scores_of(queries[head], key_buf[ctx]), -huge_value)
        top = jnp.max(scores, axis=1, keepdims=True)
        weights = jnp.exp2((scores - top) * SCORE_SCALE)
        total = jnp.sum(weights, axis=1, keepdims=True)
        acc = jnp.dot(
            weights.astype(jnp.bfloat16), value_buf[ctx], preferred_element_type=jnp.float32
        )
        keep(head, (top, total, acc))

    def source_step(source, carried):
        for head in range(heads):
            state = (top_out[head][:, :1], total_out[head][:, :1], acc_out[head])
            scores = scores_of(queries[head], key_buf[source])
            keep(head, softmax_step(state, scores, value_buf[source]))
        return carried

    lax.fori_loop(0, ctx, source_step, 0)


def page_kernel(
    page_table, page_counts, queries, own, other, top_in, total_in, acc_in,
    out, cache_out, key_buf, value_buf, zero_buf, sems, cache_sems,
):
    ctx = lax.axis_index("ctx")
    core = lax.axis_index("tp") % 2
    heads, rows, _ = queries.shape
    chunk = 1024
    zero_buf[...] = jnp.zeros_like(zero_buf)
    load_pair(own, other, key_buf, value_buf, sems, lambda copy: copy.start())
    load_pair(own, other, key_buf, value_buf, sems, lambda copy: copy.wait())

    def cache_copy(slot, source):
        return pltpu.make_async_copy(
            source, cache_out.at[pl.ds(slot * PAGE, PAGE)], cache_sems.at[slot]
        )

    for slot in range(SOURCES):
        live = page_counts[ctx, slot] > 0
        start = pl.multiple_of(page_table[ctx, slot] * PAGE, PAGE)

        @pl.when(jnp.logical_and(live, core == 0))
        def _():
            cache_copy(slot, key_buf.at[pl.ds(start, PAGE)]).start()

        @pl.when(jnp.logical_and(live, core == 1))
        def _():
            cache_copy(slot, value_buf.at[pl.ds(start, PAGE)]).start()

        @pl.when(jnp.logical_not(live))
        def _():
            cache_copy(slot, zero_buf).start()

    for head in range(heads):
        state = (top_in[head][:, :1], total_in[head][:, :1], acc_in[head])
        for at in range(0, key_buf.shape[0], chunk):
            scores = scores_of(queries[head], key_buf[at : at + chunk])
            state = softmax_step(state, scores, value_buf[at : at + chunk])
        out[:, head * HEAD_DIM : (head + 1) * HEAD_DIM] = (state[2] / state[1]).astype(jnp.bfloat16)
    for slot in range(SOURCES):
        cache_copy(slot, zero_buf).wait()


def local(stored_pages, kv_weight, page_table, page_counts, queries, turn_kv, turn_pos):
    ctx_index = lax.axis_index("ctx")
    tp_index = lax.axis_index("tp")
    core = tp_index % 2
    pair = tp_index // 8
    held, page_rows, width = stored_pages.shape
    rows = held * page_rows
    tok_new = queries.shape[0]
    heads_dev = queries.shape[1] // HEAD_DIM
    bf16 = jnp.bfloat16
    f32 = jnp.float32
    params = pltpu.CompilerParams(vmem_limit_bytes=VMEM_BYTES)

    own_x = stored_pages.reshape(rows, width)
    by_group = kv_weight.reshape(2, 4, 2, width, HEAD_DIM)

    def weight_rows(which_pair, which_core):
        picked = lax.dynamic_slice(
            by_group, (which_pair, 0, which_core, 0, 0), (1, 4, 1, width, HEAD_DIM)
        )
        return picked.reshape(4, width, HEAD_DIM)

    w2 = swapped(weight_rows(1 - pair, core), 12)
    w3 = swapped(weight_rows(1 - pair, 1 - core), 13)
    x1 = swapped(own_x, 2)
    x2 = swapped(own_x, 4)
    x3 = swapped(own_x, 6)
    w1 = swapped(weight_rows(pair, 1 - core), 1)

    local_pos = lax.dynamic_slice_in_dim(turn_pos, ctx_index * tok_new, tok_new)
    page_pos = ctx_index * rows + jnp.arange(rows, dtype=jnp.int32)
    cosine, sine = rope_tables(jnp.concatenate([local_pos, page_pos]))

    query_heads, turn_block = pl.pallas_call(
        prepare_kernel,
        out_shape=(
            jax.ShapeDtypeStruct((heads_dev, tok_new, HEAD_DIM), bf16),
            jax.ShapeDtypeStruct((SOURCES, tok_new, HEAD_DIM), bf16),
        ),
        in_specs=[vmem_spec()] * 4,
        out_specs=(vmem_spec(), vmem_spec()),
        compiler_params=params,
        name="prepare",
    )(queries, turn_kv, cosine[:tok_new], sine[:tok_new])
    own_turn = lax.all_to_all(turn_block, "ctx", split_axis=0, concat_axis=0)
    other_turn = swapped(own_turn, 1)

    state_shape = jax.ShapeDtypeStruct((heads_dev, tok_new, HEAD_DIM), f32)
    state = pl.pallas_call(
        turn_kernel,
        out_shape=(state_shape,) * 3,
        in_specs=[vmem_spec(), any_spec(), any_spec()],
        out_specs=(vmem_spec(),) * 3,
        scratch_shapes=[
            pltpu.VMEM((SOURCES, tok_new, HEAD_DIM), bf16),
            pltpu.VMEM((SOURCES, tok_new, HEAD_DIM), bf16),
            pltpu.SemaphoreType.DMA((2,)),
        ],
        compiler_params=params,
        name="turn_attention",
    )(query_heads, own_turn, other_turn)

    part_shape = jax.ShapeDtypeStruct((rows, HEAD_DIM), bf16)
    own_part, part1, part2, part3 = pl.pallas_call(
        project_kernel,
        out_shape=(jax.ShapeDtypeStruct((rows, HEAD_DIM), f32),) + (part_shape,) * 3,
        in_specs=[any_spec()] * 8,
        out_specs=(vmem_spec(),) * 4,
        scratch_shapes=[
            pltpu.VMEM((4, rows, width), bf16),
            pltpu.VMEM((4, width, 4 * HEAD_DIM), bf16),
            pltpu.SemaphoreType.DMA((4, 5)),
        ],
        compiler_params=params,
        name="project",
    )(own_x, x1, x2, x3, kv_weight, w1, w2, w3)
    got1 = swapped(part1, 1)
    got2 = swapped(part2, 12)
    got3 = swapped(part3, 13)
    own_block = pl.pallas_call(
        finish_kernel,
        out_shape=jax.ShapeDtypeStruct((SOURCES, rows, HEAD_DIM), bf16),
        in_specs=[vmem_spec()] * 6,
        out_specs=vmem_spec(),
        compiler_params=params,
        name="finish",
    )(own_part, got1, got2, got3, cosine[tok_new:], sine[tok_new:])
    own_pages = lax.all_to_all(own_block, "ctx", split_axis=0, concat_axis=0)
    own_pages = own_pages.reshape(SOURCES * rows, HEAD_DIM)
    other_pages = swapped(own_pages, 1)

    attended, cache = pl.pallas_call(
        page_kernel,
        out_shape=(
            jax.ShapeDtypeStruct((tok_new, heads_dev * HEAD_DIM), bf16),
            jax.ShapeDtypeStruct((SOURCES * PAGE, HEAD_DIM), bf16),
        ),
        in_specs=[smem_spec(), smem_spec(), vmem_spec(), any_spec(), any_spec()] + [vmem_spec()] * 3,
        out_specs=(vmem_spec(), any_spec()),
        scratch_shapes=[
            pltpu.VMEM((SOURCES * rows, HEAD_DIM), bf16),
            pltpu.VMEM((SOURCES * rows, HEAD_DIM), bf16),
            pltpu.VMEM((PAGE, HEAD_DIM), bf16),
            pltpu.SemaphoreType.DMA((2,)),
            pltpu.SemaphoreType.DMA((SOURCES,)),
        ],
        compiler_params=params,
        name="page_attention",
    )(page_table, page_counts, query_heads, own_pages, other_pages, *state)
    return (attended, cache)


def solution(mesh):
    placed = (P("ctx", None, "tp"), P(None, "tp"), P(), P(), P("ctx", "tp"), P("ctx", "tp"), P())
    return jax.shard_map(
        local,
        mesh=mesh,
        in_specs=placed,
        out_specs=(P("ctx", "tp"), P("ctx", "tp")),
        check_vma=False,
    )
```

```python
import functools
import math

import jax
import jax.numpy as jnp
from jax import lax
from jax.experimental import pallas as pl
from jax.experimental.pallas import tpu as pltpu
from jax.sharding import PartitionSpec as P

HEAD_DIM = 128
PAGE = 128
SOURCES = 8
huge_value = 1e30
SCORE_SCALE = math.log2(math.e) / math.sqrt(HEAD_DIM)
VMEM_BYTES = 32 * 1024 * 1024


def swapped(value, bits):
    return lax.ppermute(value, "tp", [(i, i ^ bits) for i in range(lax.axis_size("tp"))])


def across(value, bits):
    peers = lax.axis_size("ctx") * lax.axis_size("tp")
    flip = 4 * lax.axis_size("tp") + 2 + bits
    return lax.ppermute(value, ("ctx", "tp"), [(i, i ^ flip) for i in range(peers)])


def inverse_freq(head_width):
    half_width = head_width // 2
    exponent = jnp.arange(half_width, dtype=jnp.float32) * 2.0 / head_width
    base_freq = jnp.exp(-exponent * math.log(500000.0))
    wavelength = 2.0 * math.pi / base_freq
    smooth = (8192.0 / wavelength - 1.0) / 3.0
    blended = (1.0 - smooth) * base_freq / 8.0 + smooth * base_freq
    return jnp.where(
        wavelength < 2048.0, base_freq, jnp.where(wavelength > 8192.0, base_freq / 8.0, blended)
    )


def rope_tables(positions):
    angle = positions.astype(jnp.float32)[:, None] * inverse_freq(HEAD_DIM)[None, :]
    cosine = jnp.cos(angle)
    sine = jnp.sin(angle)
    return (
        jnp.concatenate([cosine, cosine], axis=1),
        jnp.concatenate([-sine, sine], axis=1),
    )


def turned(value, cosine, sine):
    return value * cosine + pltpu.roll(value, HEAD_DIM // 2, 1) * sine


def any_spec():
    return pl.BlockSpec(memory_space=pl.ANY)


def vmem_spec():
    return pl.BlockSpec(memory_space=pltpu.VMEM)


def smem_spec():
    return pl.BlockSpec(memory_space=pltpu.SMEM)


def prepare_kernel(queries, turn_kv, cosine, sine, query_out, turn_out):
    is_key = lax.axis_index("tp") % 2 == 0
    c = cosine[...]
    s = sine[...]
    for head in range(query_out.shape[0]):
        block = queries[:, head * HEAD_DIM : (head + 1) * HEAD_DIM].astype(jnp.float32)
        query_out[head] = turned(block, c, s).astype(jnp.bfloat16)
    block = turn_kv[...].astype(jnp.float32)
    block = turned(block, jnp.where(is_key, c, 1.0), jnp.where(is_key, s, 0.0)).astype(jnp.bfloat16)
    for peer in range(SOURCES):
        turn_out[peer] = block


def project_kernel(x0, x1, x2, x3, weight, w1, w2, w3, own_out, out1, out2, out3, x_buf, w_buf, sems):
    tp = lax.axis_index("tp")
    low = tp % 4
    spot = tp // 4
    depth = x_buf.shape[2]
    copies = []
    for r, x in enumerate((x0, x1, x2, x3)):
        at = spot ^ r
        row = (at * 4 + low) * depth
        group = [pltpu.make_async_copy(x, x_buf.at[r], sems.at[r, 0])]
        group.append(
            pltpu.make_async_copy(
                weight.at[pl.ds(pl.multiple_of(row, depth), depth)],
                w_buf.at[r, :, pl.ds(0, HEAD_DIM)],
                sems.at[r, 1],
            )
        )
        for b, w in enumerate((w1, w2, w3)):
            group.append(
                pltpu.make_async_copy(
                    w.at[at], w_buf.at[r, :, pl.ds((b + 1) * HEAD_DIM, HEAD_DIM)], sems.at[r, b + 2]
                )
            )
        for copy in group:
            copy.start()
        copies.append(group)
    total = None
    for r in range(4):
        for copy in copies[r]:
            copy.wait()
        part = jnp.dot(x_buf[r], w_buf[r], preferred_element_type=jnp.float32)
        total = part if total is None else total + part
    own_out[...] = total[:, :HEAD_DIM]
    for b, out in enumerate((out1, out2, out3)):
        out[...] = total[:, (b + 1) * HEAD_DIM : (b + 2) * HEAD_DIM].astype(jnp.bfloat16)


def finish_kernel(own, p1, p2, p3, cosine, sine, out):
    is_key = lax.axis_index("tp") % 2 == 0
    value = own[...] + p1[...].astype(jnp.float32)
    value = value + (p2[...].astype(jnp.float32) + p3[...].astype(jnp.float32))
    c = jnp.where(is_key, cosine[...], 1.0)
    s = jnp.where(is_key, sine[...], 0.0)
    block = turned(value, c, s).astype(jnp.bfloat16)
    for peer in range(SOURCES):
        out[peer] = block


def scores_of(query, keys):
    return lax.dot_general(
        query, keys, (((1,), (1,)), ((), ())), preferred_element_type=jnp.float32
    )


def softmax_step(state, scores, values):
    top, total, acc = state
    new_top = jnp.maximum(top, jnp.max(scores, axis=1, keepdims=True))
    decay = jnp.exp2((top - new_top) * SCORE_SCALE)
    weights = jnp.exp2((scores - new_top) * SCORE_SCALE)
    total = total * decay + jnp.sum(weights, axis=1, keepdims=True)
    acc = acc * decay + jnp.dot(
        weights.astype(jnp.bfloat16), values, preferred_element_type=jnp.float32
    )
    return new_top, total, acc


def load_pair(own, other, key_buf, value_buf, sems, act):
    core = lax.axis_index("tp") % 2

    @pl.when(core == 0)
    def _():
        act(pltpu.make_async_copy(own, key_buf, sems.at[0]))
        act(pltpu.make_async_copy(other, value_buf, sems.at[1]))

    @pl.when(core == 1)
    def _():
        act(pltpu.make_async_copy(other, key_buf, sems.at[0]))
        act(pltpu.make_async_copy(own, value_buf, sems.at[1]))


def turn_kernel(queries, own, other, top_out, total_out, acc_out, key_buf, value_buf, sems):
    ctx = lax.axis_index("ctx")
    heads, rows, _ = queries.shape
    load_pair(own, other, key_buf, value_buf, sems, lambda copy: copy.start())
    load_pair(own, other, key_buf, value_buf, sems, lambda copy: copy.wait())
    stacked = queries[...].reshape(heads * rows, HEAD_DIM)
    shape = (heads * rows, rows)
    token = lax.broadcasted_iota(jnp.int32, shape, 0) % rows
    seen = lax.broadcasted_iota(jnp.int32, shape, 1) <= token

    def keep(state):
        top, total, acc = state
        top_out[...] = jnp.broadcast_to(top, top_out.shape)
        total_out[...] = jnp.broadcast_to(total, total_out.shape)
        acc_out[...] = acc

    scores = jnp.where(seen, scores_of(stacked, key_buf[ctx]), -huge_value)
    top = jnp.max(scores, axis=1, keepdims=True)
    weights = jnp.exp2((scores - top) * SCORE_SCALE)
    total = jnp.sum(weights, axis=1, keepdims=True)
    acc = jnp.dot(weights.astype(jnp.bfloat16), value_buf[ctx], preferred_element_type=jnp.float32)
    keep((top, total, acc))

    def source_step(source, carried):
        state = (top_out[:, :1], total_out[:, :1], acc_out[...])
        keep(softmax_step(state, scores_of(stacked, key_buf[source]), value_buf[source]))
        return carried

    lax.fori_loop(0, ctx, source_step, 0)


def page_kernel(
    page_table, page_counts, queries, own, other, top_in, total_in, acc_in,
    out, cache_out, key_buf, value_buf, zero_buf, sems, cache_sems,
):
    ctx = lax.axis_index("ctx")
    core = lax.axis_index("tp") % 2
    heads, rows, _ = queries.shape
    chunk = 512
    zero_buf[...] = jnp.zeros_like(zero_buf)
    load_pair(own, other, key_buf, value_buf, sems, lambda copy: copy.start())
    load_pair(own, other, key_buf, value_buf, sems, lambda copy: copy.wait())

    def cache_copy(slot, source):
        return pltpu.make_async_copy(
            source, cache_out.at[pl.ds(slot * PAGE, PAGE)], cache_sems.at[slot]
        )

    for slot in range(SOURCES):
        live = page_counts[ctx, slot] > 0
        start = pl.multiple_of(page_table[ctx, slot] * PAGE, PAGE)

        @pl.when(jnp.logical_and(live, core == 0))
        def _():
            cache_copy(slot, key_buf.at[pl.ds(start, PAGE)]).start()

        @pl.when(jnp.logical_and(live, core == 1))
        def _():
            cache_copy(slot, value_buf.at[pl.ds(start, PAGE)]).start()

        @pl.when(jnp.logical_not(live))
        def _():
            cache_copy(slot, zero_buf).start()

    stacked = queries[...].reshape(heads * rows, HEAD_DIM)
    state = (top_in[:, :1], total_in[:, :1], acc_in[...])
    for at in range(0, key_buf.shape[0], chunk):
        scores = scores_of(stacked, key_buf[at : at + chunk])
        state = softmax_step(state, scores, value_buf[at : at + chunk])
    result = (state[2] / state[1]).astype(jnp.bfloat16)
    for head in range(heads):
        out[:, head * HEAD_DIM : (head + 1) * HEAD_DIM] = result[head * rows : (head + 1) * rows]
    for slot in range(SOURCES):
        cache_copy(slot, zero_buf).wait()


def local(stored_pages, kv_weight, page_table, page_counts, queries, turn_kv, turn_pos):
    ctx_index = lax.axis_index("ctx")
    tp_index = lax.axis_index("tp")
    held, page_rows, width = stored_pages.shape
    rows = held * page_rows
    tok_new = queries.shape[0]
    heads_dev = queries.shape[1] // HEAD_DIM
    bf16 = jnp.bfloat16
    f32 = jnp.float32
    params = pltpu.CompilerParams(vmem_limit_bytes=VMEM_BYTES)

    own_x = stored_pages.reshape(rows, width)
    by_group = kv_weight.reshape(4, 4, width, HEAD_DIM)

    def weight_rows(bits):
        picked = lax.dynamic_slice_in_dim(by_group, (tp_index % 4) ^ bits, 1, axis=1)
        return picked.reshape(4, width, HEAD_DIM)

    w2 = across(weight_rows(2), 0)
    w3 = across(weight_rows(3), 1)
    x1 = swapped(own_x, 4)
    x2 = swapped(own_x, 8)
    x3 = swapped(own_x, 12)
    w1 = swapped(weight_rows(1), 1)

    local_pos = lax.dynamic_slice_in_dim(turn_pos, ctx_index * tok_new, tok_new)
    page_pos = ctx_index * rows + jnp.arange(rows, dtype=jnp.int32)
    cosine, sine = rope_tables(jnp.concatenate([local_pos, page_pos]))

    query_heads, turn_block = pl.pallas_call(
        prepare_kernel,
        out_shape=(
            jax.ShapeDtypeStruct((heads_dev, tok_new, HEAD_DIM), bf16),
            jax.ShapeDtypeStruct((SOURCES, tok_new, HEAD_DIM), bf16),
        ),
        in_specs=[vmem_spec()] * 4,
        out_specs=(vmem_spec(), vmem_spec()),
        compiler_params=params,
        name="prepare",
    )(queries, turn_kv, cosine[:tok_new], sine[:tok_new])
    own_turn = lax.all_to_all(turn_block, "ctx", split_axis=0, concat_axis=0)
    other_turn = swapped(own_turn, 1)
    own_turn, other_turn, own_x = lax.optimization_barrier((own_turn, other_turn, own_x))

    state_shape = jax.ShapeDtypeStruct((heads_dev * tok_new, HEAD_DIM), f32)
    state = pl.pallas_call(
        turn_kernel,
        out_shape=(state_shape,) * 3,
        in_specs=[vmem_spec(), any_spec(), any_spec()],
        out_specs=(vmem_spec(),) * 3,
        scratch_shapes=[
            pltpu.VMEM((SOURCES, tok_new, HEAD_DIM), bf16),
            pltpu.VMEM((SOURCES, tok_new, HEAD_DIM), bf16),
            pltpu.SemaphoreType.DMA((2,)),
        ],
        compiler_params=params,
        name="turn_attention",
    )(query_heads, own_turn, other_turn)

    part_shape = jax.ShapeDtypeStruct((rows, HEAD_DIM), bf16)
    own_part, part1, part2, part3 = pl.pallas_call(
        project_kernel,
        out_shape=(jax.ShapeDtypeStruct((rows, HEAD_DIM), f32),) + (part_shape,) * 3,
        in_specs=[any_spec()] * 8,
        out_specs=(vmem_spec(),) * 4,
        scratch_shapes=[
            pltpu.VMEM((4, rows, width), bf16),
            pltpu.VMEM((4, width, 4 * HEAD_DIM), bf16),
            pltpu.SemaphoreType.DMA((4, 5)),
        ],
        compiler_params=params,
        name="project",
    )(own_x, x1, x2, x3, kv_weight, w1, w2, w3)
    got1 = swapped(part1, 1)
    got2 = swapped(part2, 2)
    got3 = swapped(part3, 3)
    own_block = pl.pallas_call(
        finish_kernel,
        out_shape=jax.ShapeDtypeStruct((SOURCES, rows, HEAD_DIM), bf16),
        in_specs=[vmem_spec()] * 6,
        out_specs=vmem_spec(),
        compiler_params=params,
        name="finish",
    )(own_part, got1, got2, got3, cosine[tok_new:], sine[tok_new:])
    own_pages = lax.all_to_all(own_block, "ctx", split_axis=0, concat_axis=0)
    own_pages = own_pages.reshape(SOURCES * rows, HEAD_DIM)
    other_pages = swapped(own_pages, 1)

    attended, cache = pl.pallas_call(
        page_kernel,
        out_shape=(
            jax.ShapeDtypeStruct((tok_new, heads_dev * HEAD_DIM), bf16),
            jax.ShapeDtypeStruct((SOURCES * PAGE, HEAD_DIM), bf16),
        ),
        in_specs=[smem_spec(), smem_spec(), vmem_spec(), any_spec(), any_spec()] + [vmem_spec()] * 3,
        out_specs=(vmem_spec(), any_spec()),
        scratch_shapes=[
            pltpu.VMEM((SOURCES * rows, HEAD_DIM), bf16),
            pltpu.VMEM((SOURCES * rows, HEAD_DIM), bf16),
            pltpu.VMEM((PAGE, HEAD_DIM), bf16),
            pltpu.SemaphoreType.DMA((2,)),
            pltpu.SemaphoreType.DMA((SOURCES,)),
        ],
        compiler_params=params,
        name="page_attention",
    )(page_table, page_counts, query_heads, own_pages, other_pages, *state)
    return (attended, cache)


def solution(mesh):
    placed = (P("ctx", None, "tp"), P(None, "tp"), P(), P(), P("ctx", "tp"), P("ctx", "tp"), P())
    return jax.shard_map(
        local,
        mesh=mesh,
        in_specs=placed,
        out_specs=(P("ctx", "tp"), P("ctx", "tp")),
        check_vma=False,
    )
```

```python
import functools
import math

import jax
import jax.numpy as jnp
from jax import lax
from jax.experimental import pallas as pl
from jax.experimental.pallas import tpu as pltpu
from jax.sharding import PartitionSpec as P

HEAD_DIM = 128
PAGE = 128
SOURCES = 8
huge_value = 1e30
SCORE_SCALE = math.log2(math.e) / math.sqrt(HEAD_DIM)
VMEM_BYTES = 32 * 1024 * 1024


def swapped(value, bits):
    return lax.ppermute(value, "tp", [(i, i ^ bits) for i in range(lax.axis_size("tp"))])


def across(value, bits):
    peers = lax.axis_size("ctx") * lax.axis_size("tp")
    flip = 4 * lax.axis_size("tp") + 2 + bits
    return lax.ppermute(value, ("ctx", "tp"), [(i, i ^ flip) for i in range(peers)])


def inverse_freq(head_width):
    half_width = head_width // 2
    exponent = jnp.arange(half_width, dtype=jnp.float32) * 2.0 / head_width
    base_freq = jnp.exp(-exponent * math.log(500000.0))
    wavelength = 2.0 * math.pi / base_freq
    smooth = (8192.0 / wavelength - 1.0) / 3.0
    blended = (1.0 - smooth) * base_freq / 8.0 + smooth * base_freq
    return jnp.where(
        wavelength < 2048.0, base_freq, jnp.where(wavelength > 8192.0, base_freq / 8.0, blended)
    )


def rope_tables(positions):
    angle = positions.astype(jnp.float32)[:, None] * inverse_freq(HEAD_DIM)[None, :]
    cosine = jnp.cos(angle)
    sine = jnp.sin(angle)
    return (
        jnp.concatenate([cosine, cosine], axis=1),
        jnp.concatenate([-sine, sine], axis=1),
    )


def turned(value, cosine, sine):
    return value * cosine + pltpu.roll(value, HEAD_DIM // 2, 1) * sine


def any_spec():
    return pl.BlockSpec(memory_space=pl.ANY)


def vmem_spec():
    return pl.BlockSpec(memory_space=pltpu.VMEM)


def smem_spec():
    return pl.BlockSpec(memory_space=pltpu.SMEM)


def prepare_kernel(queries, turn_kv, cosine, sine, query_out, turn_out):
    is_key = lax.axis_index("tp") % 2 == 0
    c = cosine[...]
    s = sine[...]
    for head in range(query_out.shape[0]):
        block = queries[:, head * HEAD_DIM : (head + 1) * HEAD_DIM].astype(jnp.float32)
        query_out[head] = turned(block, c, s).astype(jnp.bfloat16)
    block = turn_kv[...].astype(jnp.float32)
    block = turned(block, jnp.where(is_key, c, 1.0), jnp.where(is_key, s, 0.0)).astype(jnp.bfloat16)
    turn_out[...] = block


def project_kernel(x0, x1, x2, x3, weight, w1, w2, w3, own_out, out1, out2, out3, x_buf, w_buf, sems):
    tp = lax.axis_index("tp")
    low = tp % 4
    spot = tp // 4
    depth = x_buf.shape[2]
    copies = []
    for r, x in enumerate((x0, x1, x2, x3)):
        at = spot ^ r
        row = (at * 4 + low) * depth
        group = [pltpu.make_async_copy(x, x_buf.at[r], sems.at[r, 0])]
        group.append(
            pltpu.make_async_copy(
                weight.at[pl.ds(pl.multiple_of(row, depth), depth)],
                w_buf.at[r, :, pl.ds(0, HEAD_DIM)],
                sems.at[r, 1],
            )
        )
        for b, w in enumerate((w1, w2, w3)):
            group.append(
                pltpu.make_async_copy(
                    w.at[at], w_buf.at[r, :, pl.ds((b + 1) * HEAD_DIM, HEAD_DIM)], sems.at[r, b + 2]
                )
            )
        for copy in group:
            copy.start()
        copies.append(group)
    total = None
    for r in range(4):
        for copy in copies[r]:
            copy.wait()
        part = jnp.dot(x_buf[r], w_buf[r], preferred_element_type=jnp.float32)
        total = part if total is None else total + part
    own_out[...] = total[:, :HEAD_DIM]
    for b, out in enumerate((out1, out2, out3)):
        out[...] = total[:, (b + 1) * HEAD_DIM : (b + 2) * HEAD_DIM].astype(jnp.bfloat16)


def finish_kernel(own, p1, p2, p3, cosine, sine, out):
    is_key = lax.axis_index("tp") % 2 == 0
    value = own[...] + p1[...].astype(jnp.float32)
    value = value + (p2[...].astype(jnp.float32) + p3[...].astype(jnp.float32))
    c = jnp.where(is_key, cosine[...], 1.0)
    s = jnp.where(is_key, sine[...], 0.0)
    block = turned(value, c, s).astype(jnp.bfloat16)
    for peer in range(SOURCES):
        out[peer] = block


def scores_of(query, keys):
    return lax.dot_general(
        query, keys, (((1,), (1,)), ((), ())), preferred_element_type=jnp.float32
    )


def widened(value, width):
    return value if width == HEAD_DIM else jnp.concatenate([value] * (width // HEAD_DIM), axis=1)


def softmax_step(state, scores, values):
    top, total, acc = state
    width = scores.shape[1]
    new_top = jnp.maximum(top, jnp.max(scores, axis=1, keepdims=True))
    decay = jnp.exp2((top - new_top) * SCORE_SCALE)
    weights = jnp.exp2((scores - widened(new_top, width)) * SCORE_SCALE)
    total = total * decay
    for at in range(0, width, HEAD_DIM):
        total = total + weights[:, at : at + HEAD_DIM]
    acc = acc * decay + jnp.dot(
        weights.astype(jnp.bfloat16), values, preferred_element_type=jnp.float32
    )
    return new_top, total, acc


def load_pair(own, other, key_buf, value_buf, sems, act):
    core = lax.axis_index("tp") % 2

    @pl.when(core == 0)
    def _():
        act(pltpu.make_async_copy(own, key_buf, sems.at[0]))
        act(pltpu.make_async_copy(other, value_buf, sems.at[1]))

    @pl.when(core == 1)
    def _():
        act(pltpu.make_async_copy(other, key_buf, sems.at[0]))
        act(pltpu.make_async_copy(own, value_buf, sems.at[1]))


def turn_kernel(queries, pairs, top_out, total_out, acc_out):
    ctx = lax.axis_index("ctx")
    core = lax.axis_index("tp") % 2
    heads, rows, _ = queries.shape
    stacked = queries[...].reshape(heads * rows, HEAD_DIM)
    shape = (heads * rows, rows)
    token = lax.broadcasted_iota(jnp.int32, shape, 0) % rows
    seen = lax.broadcasted_iota(jnp.int32, shape, 1) <= token

    def keep(state):
        top_out[...], total_out[...], acc_out[...] = state

    none = jnp.zeros(top_out.shape, jnp.float32)
    scores = jnp.where(seen, scores_of(stacked, pairs[ctx, core]), -huge_value)
    keep(softmax_step((none - huge_value, none, none), scores, pairs[ctx, 1 - core]))

    def source_step(source, carried):
        state = (top_out[...], total_out[...], acc_out[...])
        scores = scores_of(stacked, pairs[source, core])
        keep(softmax_step(state, scores, pairs[source, 1 - core]))
        return carried

    lax.fori_loop(0, ctx, source_step, 0)


def page_kernel(
    page_table, page_counts, queries, own, other, top_in, total_in, acc_in,
    out, cache_out, key_buf, value_buf, zero_buf, sems, cache_sems,
):
    ctx = lax.axis_index("ctx")
    core = lax.axis_index("tp") % 2
    heads, rows, _ = queries.shape
    chunk = 512
    zero_buf[...] = jnp.zeros_like(zero_buf)
    load_pair(own, other, key_buf, value_buf, sems, lambda copy: copy.start())
    load_pair(own, other, key_buf, value_buf, sems, lambda copy: copy.wait())

    def cache_copy(slot, source):
        return pltpu.make_async_copy(
            source, cache_out.at[pl.ds(slot * PAGE, PAGE)], cache_sems.at[slot]
        )

    for slot in range(SOURCES):
        live = page_counts[ctx, slot] > 0
        start = pl.multiple_of(page_table[ctx, slot] * PAGE, PAGE)

        @pl.when(jnp.logical_and(live, core == 0))
        def _():
            cache_copy(slot, key_buf.at[pl.ds(start, PAGE)]).start()

        @pl.when(jnp.logical_and(live, core == 1))
        def _():
            cache_copy(slot, value_buf.at[pl.ds(start, PAGE)]).start()

        @pl.when(jnp.logical_not(live))
        def _():
            cache_copy(slot, zero_buf).start()

    stacked = queries[...].reshape(heads * rows, HEAD_DIM)
    state = (top_in[...], total_in[...], acc_in[...])
    for at in range(0, key_buf.shape[0], chunk):
        scores = scores_of(stacked, key_buf[at : at + chunk])
        state = softmax_step(state, scores, value_buf[at : at + chunk])
    result = (state[2] / jnp.sum(state[1], axis=1, keepdims=True)).astype(jnp.bfloat16)
    for head in range(heads):
        out[:, head * HEAD_DIM : (head + 1) * HEAD_DIM] = result[head * rows : (head + 1) * rows]
    for slot in range(SOURCES):
        cache_copy(slot, zero_buf).wait()


def local(stored_pages, kv_weight, page_table, page_counts, queries, turn_kv, turn_pos):
    ctx_index = lax.axis_index("ctx")
    tp_index = lax.axis_index("tp")
    held, page_rows, width = stored_pages.shape
    rows = held * page_rows
    tok_new = queries.shape[0]
    heads_dev = queries.shape[1] // HEAD_DIM
    bf16 = jnp.bfloat16
    f32 = jnp.float32
    params = pltpu.CompilerParams(vmem_limit_bytes=VMEM_BYTES)

    own_x = stored_pages.reshape(rows, width)
    by_group = kv_weight.reshape(4, 4, width, HEAD_DIM)

    def weight_rows(bits):
        picked = lax.dynamic_slice_in_dim(by_group, (tp_index % 4) ^ bits, 1, axis=1)
        return picked.reshape(4, width, HEAD_DIM)

    w2 = across(weight_rows(2), 0)
    w3 = across(weight_rows(3), 1)
    x1 = swapped(own_x, 4)
    x2 = swapped(own_x, 8)
    x3 = swapped(own_x, 12)
    w1 = swapped(weight_rows(1), 1)

    local_pos = lax.dynamic_slice_in_dim(turn_pos, ctx_index * tok_new, tok_new)
    page_pos = ctx_index * rows + jnp.arange(rows, dtype=jnp.int32)
    cosine, sine = rope_tables(jnp.concatenate([local_pos, page_pos]))

    query_heads, turn_block = pl.pallas_call(
        prepare_kernel,
        out_shape=(
            jax.ShapeDtypeStruct((heads_dev, tok_new, HEAD_DIM), bf16),
            jax.ShapeDtypeStruct((tok_new, HEAD_DIM), bf16),
        ),
        in_specs=[vmem_spec()] * 4,
        out_specs=(vmem_spec(), vmem_spec()),
        compiler_params=params,
        name="prepare",
    )(queries, turn_kv, cosine[:tok_new], sine[:tok_new])
    pair = jnp.stack([turn_block, swapped(turn_block, 1)])
    turn_pairs = lax.all_gather(pair, "ctx", axis=0)

    part_shape = jax.ShapeDtypeStruct((rows, HEAD_DIM), bf16)
    own_part, part1, part2, part3 = pl.pallas_call(
        project_kernel,
        out_shape=(jax.ShapeDtypeStruct((rows, HEAD_DIM), f32),) + (part_shape,) * 3,
        in_specs=[any_spec()] * 8,
        out_specs=(vmem_spec(),) * 4,
        scratch_shapes=[
            pltpu.VMEM((4, rows, width), bf16),
            pltpu.VMEM((4, width, 4 * HEAD_DIM), bf16),
            pltpu.SemaphoreType.DMA((4, 5)),
        ],
        compiler_params=params,
        name="project",
    )(own_x, x1, x2, x3, kv_weight, w1, w2, w3)
    got1 = swapped(part1, 1)
    got2 = swapped(part2, 2)
    got3 = swapped(part3, 3)
    own_block = pl.pallas_call(
        finish_kernel,
        out_shape=jax.ShapeDtypeStruct((SOURCES, rows, HEAD_DIM), bf16),
        in_specs=[vmem_spec()] * 6,
        out_specs=vmem_spec(),
        compiler_params=params,
        name="finish",
    )(own_part, got1, got2, got3, cosine[tok_new:], sine[tok_new:])
    own_block, turn_pairs = lax.optimization_barrier((own_block, turn_pairs))
    own_pages = lax.all_to_all(own_block, "ctx", split_axis=0, concat_axis=0)
    state_shape = jax.ShapeDtypeStruct((heads_dev * tok_new, HEAD_DIM), f32)
    state = pl.pallas_call(
        turn_kernel,
        out_shape=(state_shape,) * 3,
        in_specs=[vmem_spec()] * 2,
        out_specs=(vmem_spec(),) * 3,
        compiler_params=params,
        cost_estimate=pl.CostEstimate(
            flops=8 * heads_dev * tok_new * tok_new * SOURCES * HEAD_DIM,
            bytes_accessed=6 * 1024 * 1024,
            transcendentals=heads_dev * tok_new * tok_new * SOURCES,
        ),
        name="turn_attention",
    )(query_heads, turn_pairs)
    own_pages, state = lax.optimization_barrier((own_pages, state))
    own_pages = own_pages.reshape(SOURCES * rows, HEAD_DIM)
    other_pages = swapped(own_pages, 1)

    attended, cache = pl.pallas_call(
        page_kernel,
        out_shape=(
            jax.ShapeDtypeStruct((tok_new, heads_dev * HEAD_DIM), bf16),
            jax.ShapeDtypeStruct((SOURCES * PAGE, HEAD_DIM), bf16),
        ),
        in_specs=[smem_spec(), smem_spec(), vmem_spec(), any_spec(), any_spec()] + [vmem_spec()] * 3,
        out_specs=(vmem_spec(), any_spec()),
        scratch_shapes=[
            pltpu.VMEM((SOURCES * rows, HEAD_DIM), bf16),
            pltpu.VMEM((SOURCES * rows, HEAD_DIM), bf16),
            pltpu.VMEM((PAGE, HEAD_DIM), bf16),
            pltpu.SemaphoreType.DMA((2,)),
            pltpu.SemaphoreType.DMA((SOURCES,)),
        ],
        compiler_params=params,
        name="page_attention",
    )(page_table, page_counts, query_heads, own_pages, other_pages, *state)
    return (attended, cache)


def solution(mesh):
    placed = (P("ctx", None, "tp"), P(None, "tp"), P(), P(), P("ctx", "tp"), P("ctx", "tp"), P())
    return jax.shard_map(
        local,
        mesh=mesh,
        in_specs=placed,
        out_specs=(P("ctx", "tp"), P("ctx", "tp")),
        check_vma=False,
    )
```

```python
import functools
import math

import jax
import jax.numpy as jnp
from jax import lax
from jax.experimental import pallas as pl
from jax.experimental.pallas import tpu as pltpu
from jax.sharding import PartitionSpec as P

HEAD_DIM = 128
PAGE = 128
SOURCES = 8
huge_value = 1e30
SCORE_SCALE = math.log2(math.e) / math.sqrt(HEAD_DIM)
VMEM_BYTES = 32 * 1024 * 1024


def swapped(value, bits):
    return lax.ppermute(value, "tp", [(i, i ^ bits) for i in range(lax.axis_size("tp"))])


def across(value):
    peers = lax.axis_size("ctx") * lax.axis_size("tp")
    flip = 4 * lax.axis_size("tp") + 2
    return lax.ppermute(value, ("ctx", "tp"), [(i, i ^ flip) for i in range(peers)])


def inverse_freq(head_width):
    half_width = head_width // 2
    exponent = jnp.arange(half_width, dtype=jnp.float32) * 2.0 / head_width
    base_freq = jnp.exp(-exponent * math.log(500000.0))
    wavelength = 2.0 * math.pi / base_freq
    smooth = (8192.0 / wavelength - 1.0) / 3.0
    blended = (1.0 - smooth) * base_freq / 8.0 + smooth * base_freq
    return jnp.where(
        wavelength < 2048.0, base_freq, jnp.where(wavelength > 8192.0, base_freq / 8.0, blended)
    )


def rope_tables(positions):
    angle = positions.astype(jnp.float32)[:, None] * inverse_freq(HEAD_DIM)[None, :]
    cosine = jnp.cos(angle)
    sine = jnp.sin(angle)
    return (
        jnp.concatenate([cosine, cosine], axis=1),
        jnp.concatenate([-sine, sine], axis=1),
    )


def turned(value, cosine, sine):
    return value * cosine + pltpu.roll(value, HEAD_DIM // 2, 1) * sine


def any_spec():
    return pl.BlockSpec(memory_space=pl.ANY)


def vmem_spec():
    return pl.BlockSpec(memory_space=pltpu.VMEM)


def smem_spec():
    return pl.BlockSpec(memory_space=pltpu.SMEM)


def prepare_kernel(queries, turn_kv, cosine, sine, query_out, turn_out):
    is_key = lax.axis_index("tp") % 2 == 0
    c = cosine[...]
    s = sine[...]
    for head in range(query_out.shape[0]):
        block = queries[:, head * HEAD_DIM : (head + 1) * HEAD_DIM].astype(jnp.float32)
        query_out[head] = turned(block, c, s).astype(jnp.bfloat16)
    block = turn_kv[...].astype(jnp.float32)
    block = turned(block, jnp.where(is_key, c, 1.0), jnp.where(is_key, s, 0.0)).astype(jnp.bfloat16)
    for peer in range(SOURCES):
        turn_out[peer] = block


def project_kernel(*refs):
    slices, (weight, far_weight, own_out, far_out, x_buf, w_buf, sems) = refs[:10], refs[10:]
    tp = lax.axis_index("tp")
    low = tp % 4
    spot = tp // 4
    depth = slices[0].shape[1]
    rows = x_buf.shape[1]
    copies = []
    for i, r in enumerate((0, 1, 3, 2)):
        at = spot ^ r
        for half in range(2):
            part = pl.ds(half * depth, depth)
            core = (low % 2) ^ half
            near_row = pl.multiple_of((at * 4 + (low ^ half)) * depth, depth)
            far_row = pl.multiple_of(core * depth, depth)
            group = [
                pltpu.make_async_copy(
                    weight.at[pl.ds(near_row, depth)],
                    w_buf.at[r, part, pl.ds(0, HEAD_DIM)],
                    sems.at[r, half, 0],
                ),
                pltpu.make_async_copy(
                    far_weight.at[at, pl.ds(far_row, depth)],
                    w_buf.at[r, part, pl.ds(HEAD_DIM, HEAD_DIM)],
                    sems.at[r, half, 1],
                ),
            ]
            sent = [(slices[2 * i + half], 0, rows)]
            if r == 2:
                sent = [(slices[6 + half], 0, rows // 2), (slices[8 + half], rows // 2, rows // 2)]
            for k, (piece, first, count) in enumerate(sent):
                place = x_buf.at[r, pl.ds(first, count), part]
                group.append(pltpu.make_async_copy(piece, place, sems.at[r, half, 2 + k]))
            for copy in group:
                copy.start()
            copies.append(group)
    total = None
    for i, r in enumerate((0, 1, 3, 2)):
        for copy in copies[2 * i] + copies[2 * i + 1]:
            copy.wait()
        part = jnp.dot(x_buf[r], w_buf[r], preferred_element_type=jnp.float32)
        total = part if total is None else total + part
    own_out[...] = total[:, :HEAD_DIM]
    far_out[...] = total[:, HEAD_DIM:].astype(jnp.bfloat16)


def finish_kernel(own, far, cosine, sine, out):
    is_key = lax.axis_index("tp") % 2 == 0
    value = own[...] + far[...].astype(jnp.float32)
    c = jnp.where(is_key, cosine[...], 1.0)
    s = jnp.where(is_key, sine[...], 0.0)
    block = turned(value, c, s).astype(jnp.bfloat16)
    for peer in range(SOURCES):
        out[peer] = block


def scores_of(query, keys):
    return lax.dot_general(
        query, keys, (((1,), (1,)), ((), ())), preferred_element_type=jnp.float32
    )


def widened(value, width):
    return value if width == HEAD_DIM else jnp.concatenate([value] * (width // HEAD_DIM), axis=1)


def softmax_step(state, scores, values):
    top, total, acc = state
    width = scores.shape[1]
    new_top = jnp.maximum(top, jnp.max(scores, axis=1, keepdims=True))
    decay = jnp.exp2((top - new_top) * SCORE_SCALE)
    weights = jnp.exp2((scores - widened(new_top, width)) * SCORE_SCALE)
    total = total * decay
    for at in range(0, width, HEAD_DIM):
        total = total + weights[:, at : at + HEAD_DIM]
    acc = acc * decay + jnp.dot(
        weights.astype(jnp.bfloat16), values, preferred_element_type=jnp.float32
    )
    return new_top, total, acc


def load_pair(own, other, key_buf, value_buf, sems, act):
    core = lax.axis_index("tp") % 2

    @pl.when(core == 0)
    def _():
        act(pltpu.make_async_copy(own, key_buf, sems.at[0]))
        act(pltpu.make_async_copy(other, value_buf, sems.at[1]))

    @pl.when(core == 1)
    def _():
        act(pltpu.make_async_copy(other, key_buf, sems.at[0]))
        act(pltpu.make_async_copy(own, value_buf, sems.at[1]))


def turn_kernel(queries, own, other, top_out, total_out, acc_out):
    ctx = lax.axis_index("ctx")
    core = lax.axis_index("tp") % 2
    heads, rows, _ = queries.shape
    stacked = queries[...].reshape(heads * rows, HEAD_DIM)
    shape = (heads * rows, rows)
    token = lax.broadcasted_iota(jnp.int32, shape, 0) % rows
    seen = lax.broadcasted_iota(jnp.int32, shape, 1) <= token

    def keep(state):
        top_out[...], total_out[...], acc_out[...] = state

    none = jnp.zeros(top_out.shape, jnp.float32)

    def attend(keys, values):
        scores = jnp.where(seen, scores_of(stacked, keys[ctx]), -huge_value)
        keep(softmax_step((none - huge_value, none, none), scores, values[ctx]))

        def source_step(source, carried):
            state = (top_out[...], total_out[...], acc_out[...])
            keep(softmax_step(state, scores_of(stacked, keys[source]), values[source]))
            return carried

        lax.fori_loop(0, ctx, source_step, 0)

    pl.when(core == 0)(lambda: attend(own, other))
    pl.when(core == 1)(lambda: attend(other, own))


def page_kernel(
    page_table, page_counts, queries, own, other, top_in, total_in, acc_in,
    out, cache_out, key_buf, value_buf, zero_buf, sems, cache_sems,
):
    ctx = lax.axis_index("ctx")
    core = lax.axis_index("tp") % 2
    heads, rows, _ = queries.shape
    chunk = 512
    zero_buf[...] = jnp.zeros_like(zero_buf)
    load_pair(own, other, key_buf, value_buf, sems, lambda copy: copy.start())
    load_pair(own, other, key_buf, value_buf, sems, lambda copy: copy.wait())

    def cache_copy(slot, source):
        return pltpu.make_async_copy(
            source, cache_out.at[pl.ds(slot * PAGE, PAGE)], cache_sems.at[slot]
        )

    for slot in range(SOURCES):
        live = page_counts[ctx, slot] > 0
        start = pl.multiple_of(page_table[ctx, slot] * PAGE, PAGE)

        @pl.when(jnp.logical_and(live, core == 0))
        def _():
            cache_copy(slot, key_buf.at[pl.ds(start, PAGE)]).start()

        @pl.when(jnp.logical_and(live, core == 1))
        def _():
            cache_copy(slot, value_buf.at[pl.ds(start, PAGE)]).start()

        @pl.when(jnp.logical_not(live))
        def _():
            cache_copy(slot, zero_buf).start()

    stacked = queries[...].reshape(heads * rows, HEAD_DIM)
    state = (top_in[...], total_in[...], acc_in[...])
    for at in range(0, key_buf.shape[0], chunk):
        scores = scores_of(stacked, key_buf[at : at + chunk])
        state = softmax_step(state, scores, value_buf[at : at + chunk])
    result = (state[2] / jnp.sum(state[1], axis=1, keepdims=True)).astype(jnp.bfloat16)
    for head in range(heads):
        out[:, head * HEAD_DIM : (head + 1) * HEAD_DIM] = result[head * rows : (head + 1) * rows]
    for slot in range(SOURCES):
        cache_copy(slot, zero_buf).wait()


def local(stored_pages, kv_weight, page_table, page_counts, queries, turn_kv, turn_pos):
    ctx_index = lax.axis_index("ctx")
    tp_index = lax.axis_index("tp")
    held, page_rows, width = stored_pages.shape
    rows = held * page_rows
    tok_new = queries.shape[0]
    heads_dev = queries.shape[1] // HEAD_DIM
    bf16 = jnp.bfloat16
    f32 = jnp.float32
    params = pltpu.CompilerParams(vmem_limit_bytes=VMEM_BYTES)

    own_x = stored_pages.reshape(rows, width)
    by_half = kv_weight.reshape(4, 2, 2 * width, HEAD_DIM)
    half = (tp_index // 2) % 2
    far_rows = lax.dynamic_slice_in_dim(by_half, 1 - half, 1, axis=1)
    far_weight = across(far_rows.reshape(4, 2 * width, HEAD_DIM))
    x1 = swapped(own_x, 4)
    x3 = swapped(own_x, 12)
    x2a = swapped(x1[: rows // 2], 12)
    x2b = swapped(x3[rows // 2 :], 4)
    pieces = []
    for piece in (own_x, x1, x3, x2a, x2b):
        pieces += [piece, swapped(piece, 1)]

    local_pos = lax.dynamic_slice_in_dim(turn_pos, ctx_index * tok_new, tok_new)
    page_pos = ctx_index * rows + jnp.arange(rows, dtype=jnp.int32)
    cosine, sine = rope_tables(jnp.concatenate([local_pos, page_pos]))

    query_heads, turn_block = pl.pallas_call(
        prepare_kernel,
        out_shape=(
            jax.ShapeDtypeStruct((heads_dev, tok_new, HEAD_DIM), bf16),
            jax.ShapeDtypeStruct((SOURCES, tok_new, HEAD_DIM), bf16),
        ),
        in_specs=[vmem_spec()] * 4,
        out_specs=(vmem_spec(), vmem_spec()),
        compiler_params=params,
        name="prepare",
    )(queries, turn_kv, cosine[:tok_new], sine[:tok_new])
    turn_block, pieces[2], pieces[4] = lax.optimization_barrier((turn_block, pieces[2], pieces[4]))
    own_turn = lax.all_to_all(turn_block, "ctx", split_axis=0, concat_axis=0)
    other_turn = swapped(own_turn, 1)

    own_part, far_part = pl.pallas_call(
        project_kernel,
        out_shape=(
            jax.ShapeDtypeStruct((rows, HEAD_DIM), f32),
            jax.ShapeDtypeStruct((rows, HEAD_DIM), bf16),
        ),
        in_specs=[any_spec()] * 12,
        out_specs=(vmem_spec(),) * 2,
        scratch_shapes=[
            pltpu.VMEM((4, rows, 2 * width), bf16),
            pltpu.VMEM((4, 2 * width, 2 * HEAD_DIM), bf16),
            pltpu.SemaphoreType.DMA((4, 2, 4)),
        ],
        compiler_params=params,
        name="project",
    )(*pieces, kv_weight, far_weight)
    arrived = swapped(far_part, 2)
    own_block = pl.pallas_call(
        finish_kernel,
        out_shape=jax.ShapeDtypeStruct((SOURCES, rows, HEAD_DIM), bf16),
        in_specs=[vmem_spec()] * 4,
        out_specs=vmem_spec(),
        compiler_params=params,
        name="finish",
    )(own_part, arrived, cosine[tok_new:], sine[tok_new:])
    own_block, own_turn, other_turn = lax.optimization_barrier((own_block, own_turn, other_turn))
    own_pages = lax.all_to_all(own_block, "ctx", split_axis=0, concat_axis=0)
    state_shape = jax.ShapeDtypeStruct((heads_dev * tok_new, HEAD_DIM), f32)
    state = pl.pallas_call(
        turn_kernel,
        out_shape=(state_shape,) * 3,
        in_specs=[vmem_spec()] * 3,
        out_specs=(vmem_spec(),) * 3,
        compiler_params=params,
        cost_estimate=pl.CostEstimate(
            flops=8 * heads_dev * tok_new * tok_new * SOURCES * HEAD_DIM,
            bytes_accessed=6 * 1024 * 1024,
            transcendentals=heads_dev * tok_new * tok_new * SOURCES,
        ),
        name="turn_attention",
    )(query_heads, own_turn, other_turn)
    own_pages, state = lax.optimization_barrier((own_pages, state))
    own_pages = own_pages.reshape(SOURCES * rows, HEAD_DIM)
    other_pages = swapped(own_pages, 1)

    attended, cache = pl.pallas_call(
        page_kernel,
        out_shape=(
            jax.ShapeDtypeStruct((tok_new, heads_dev * HEAD_DIM), bf16),
            jax.ShapeDtypeStruct((SOURCES * PAGE, HEAD_DIM), bf16),
        ),
        in_specs=[smem_spec(), smem_spec(), vmem_spec(), any_spec(), any_spec()] + [vmem_spec()] * 3,
        out_specs=(vmem_spec(), any_spec()),
        scratch_shapes=[
            pltpu.VMEM((SOURCES * rows, HEAD_DIM), bf16),
            pltpu.VMEM((SOURCES * rows, HEAD_DIM), bf16),
            pltpu.VMEM((PAGE, HEAD_DIM), bf16),
            pltpu.SemaphoreType.DMA((2,)),
            pltpu.SemaphoreType.DMA((SOURCES,)),
        ],
        compiler_params=params,
        name="page_attention",
    )(page_table, page_counts, query_heads, own_pages, other_pages, *state)
    return (attended, cache)


def solution(mesh):
    placed = (P("ctx", None, "tp"), P(None, "tp"), P(), P(), P("ctx", "tp"), P("ctx", "tp"), P())
    return jax.shard_map(
        local,
        mesh=mesh,
        in_specs=placed,
        out_specs=(P("ctx", "tp"), P("ctx", "tp")),
        check_vma=False,
    )
```

```python
import functools
import math

import jax
import jax.numpy as jnp
from jax import lax
from jax.experimental import pallas as pl
from jax.experimental.pallas import tpu as pltpu
from jax.sharding import PartitionSpec as P

HEAD_DIM = 128
PAGE = 128
SOURCES = 8
huge_value = 1e30
SCORE_SCALE = math.log2(math.e) / math.sqrt(HEAD_DIM)
VMEM_BYTES = 32 * 1024 * 1024


def swapped(value, bits):
    return lax.ppermute(value, "tp", [(i, i ^ bits) for i in range(lax.axis_size("tp"))])


def shifted(value, bits):
    return lax.ppermute(value, "ctx", [(i, i ^ bits) for i in range(lax.axis_size("ctx"))])


def across(value):
    peers = lax.axis_size("ctx") * lax.axis_size("tp")
    flip = 4 * lax.axis_size("tp") + 2
    return lax.ppermute(value, ("ctx", "tp"), [(i, i ^ flip) for i in range(peers)])


def inverse_freq(head_width):
    half_width = head_width // 2
    exponent = jnp.arange(half_width, dtype=jnp.float32) * 2.0 / head_width
    base_freq = jnp.exp(-exponent * math.log(500000.0))
    wavelength = 2.0 * math.pi / base_freq
    smooth = (8192.0 / wavelength - 1.0) / 3.0
    blended = (1.0 - smooth) * base_freq / 8.0 + smooth * base_freq
    return jnp.where(
        wavelength < 2048.0, base_freq, jnp.where(wavelength > 8192.0, base_freq / 8.0, blended)
    )


def rope_tables(positions):
    angle = positions.astype(jnp.float32)[:, None] * inverse_freq(HEAD_DIM)[None, :]
    cosine = jnp.cos(angle)
    sine = jnp.sin(angle)
    return (
        jnp.concatenate([cosine, cosine], axis=1),
        jnp.concatenate([-sine, sine], axis=1),
    )


def turned(value, cosine, sine):
    return value * cosine + pltpu.roll(value, HEAD_DIM // 2, 1) * sine


def any_spec():
    return pl.BlockSpec(memory_space=pl.ANY)


def hbm_spec():
    return pl.BlockSpec(memory_space=pltpu.HBM)


def vmem_spec():
    return pl.BlockSpec(memory_space=pltpu.VMEM)


def smem_spec():
    return pl.BlockSpec(memory_space=pltpu.SMEM)


def prepare_kernel(queries, turn_kv, cosine, sine, query_out, turn_out):
    is_key = lax.axis_index("tp") % 2 == 0
    c = cosine[...]
    s = sine[...]
    for head in range(query_out.shape[0]):
        block = queries[:, head * HEAD_DIM : (head + 1) * HEAD_DIM].astype(jnp.float32)
        query_out[head] = turned(block, c, s).astype(jnp.bfloat16)
    block = turn_kv[...].astype(jnp.float32)
    block = turned(block, jnp.where(is_key, c, 1.0), jnp.where(is_key, s, 0.0)).astype(jnp.bfloat16)
    turn_out[...] = block


def pick_kernel(weight, first_out, rest_out, sems):
    odd = lax.axis_index("ctx") % 2
    far = 1 - (lax.axis_index("tp") // 2) % 2
    depth = first_out.shape[0]
    copies = []
    for i, (group, out) in enumerate(((3 * odd, first_out), (1, rest_out.at[0]), (2, rest_out.at[1]))):
        row = pl.multiple_of((group * 2 + far) * depth, depth)
        copies.append(pltpu.make_async_copy(weight.at[pl.ds(row, depth)], out, sems.at[i]))
    for copy in copies:
        copy.start()
    for copy in copies:
        copy.wait()


def project_kernel(*refs):
    slices = refs[:10]
    weight, first, rest, relayed, own_out, near_out, far_out, x_buf, w_buf, sems = refs[10:]
    odd = lax.axis_index("ctx") % 2
    tp = lax.axis_index("tp")
    low = tp % 4
    spot = tp // 4
    rows = x_buf.shape[1]
    depth = slices[0].shape[1]

    def far_copy(at, r, half, act):
        part = pl.ds(half * depth, depth)
        source = pl.ds(pl.multiple_of(((low % 2) ^ half) * depth, depth), depth)

        def go(ref):
            place = w_buf.at[r, part, pl.ds(HEAD_DIM, HEAD_DIM)]
            act(pltpu.make_async_copy(ref.at[source], place, sems.at[r, half, 1]))

        pl.when(at == 3 * odd)(lambda: go(first))
        pl.when(at == 1)(lambda: go(rest.at[0]))
        pl.when(at == 2)(lambda: go(rest.at[1]))
        pl.when(at == 3 - 3 * odd)(lambda: go(relayed))

    copies = []
    for i, r in enumerate((0, 1, 3, 2)):
        at = spot ^ r
        for half in range(2):
            part = pl.ds(half * depth, depth)
            near_row = pl.multiple_of((at * 4 + (low ^ half)) * depth, depth)
            group = [
                pltpu.make_async_copy(
                    weight.at[pl.ds(near_row, depth)],
                    w_buf.at[r, part, pl.ds(0, HEAD_DIM)],
                    sems.at[r, half, 0],
                ),
            ]
            sent = [(slices[2 * i + half], 0, rows)]
            if r == 2:
                sent = [(slices[6 + half], 0, rows // 2), (slices[8 + half], rows // 2, rows // 2)]
            for k, (piece, start, count) in enumerate(sent):
                place = x_buf.at[r, pl.ds(start, count), part]
                group.append(pltpu.make_async_copy(piece, place, sems.at[r, half, 2 + k]))
            for copy in group:
                copy.start()
            far_copy(at, r, half, lambda copy: copy.start())
            copies.append(group)
    total = None
    for i, r in enumerate((0, 1, 3, 2)):
        for half in range(2):
            for copy in copies[2 * i + half]:
                copy.wait()
            far_copy(spot ^ r, r, half, lambda copy: copy.wait())
        part = jnp.dot(x_buf[r], w_buf[r], preferred_element_type=jnp.float32)
        total = part if total is None else total + part
    own_out[...] = total[:, :HEAD_DIM]
    near_out[...] = total[:, :HEAD_DIM].astype(jnp.bfloat16)
    far_out[...] = total[:, HEAD_DIM:].astype(jnp.bfloat16)


def finish_kernel(own, p1, p2, p3, cosine, sine, out):
    is_key = lax.axis_index("tp") % 2 == 0
    rows = own.shape[0]
    mine = own[...] + p1[...].astype(jnp.float32)
    other = p2[...].astype(jnp.float32) + p3[...].astype(jnp.float32)
    for i, value in enumerate((mine, other)):
        c = jnp.where(is_key, cosine[i * rows : (i + 1) * rows], 1.0)
        s = jnp.where(is_key, sine[i * rows : (i + 1) * rows], 0.0)
        out[i * rows : (i + 1) * rows] = turned(value, c, s).astype(jnp.bfloat16)


def scores_of(query, keys):
    return lax.dot_general(
        query, keys, (((1,), (1,)), ((), ())), preferred_element_type=jnp.float32
    )


def widened(value, width):
    return value if width == HEAD_DIM else jnp.concatenate([value] * (width // HEAD_DIM), axis=1)


def softmax_step(state, scores, values):
    top, total, acc = state
    width = scores.shape[1]
    new_top = jnp.maximum(top, jnp.max(scores, axis=1, keepdims=True))
    decay = jnp.exp2((top - new_top) * SCORE_SCALE)
    weights = jnp.exp2((scores - widened(new_top, width)) * SCORE_SCALE)
    total = total * decay
    for at in range(0, width, HEAD_DIM):
        total = total + weights[:, at : at + HEAD_DIM]
    acc = acc * decay + jnp.dot(
        weights.astype(jnp.bfloat16), values, preferred_element_type=jnp.float32
    )
    return new_top, total, acc


def turn_kernel(queries, near, far, other_near, other_far, top_out, total_out, acc_out):
    ctx = lax.axis_index("ctx")
    core = lax.axis_index("tp") % 2
    heads, rows, _ = queries.shape
    stacked = queries[...].reshape(heads * rows, HEAD_DIM)
    shape = (heads * rows, rows)
    token = lax.broadcasted_iota(jnp.int32, shape, 0) % rows
    seen = lax.broadcasted_iota(jnp.int32, shape, 1) <= token

    def keep(state):
        top_out[...], total_out[...], acc_out[...] = state

    none = jnp.zeros(top_out.shape, jnp.float32)

    def attend(keys, values):
        for i in range(SOURCES):
            source = ctx ^ ((0, 4, 1, 5, 3, 7, 2, 6)[i])
            part = slice(i % 4 * rows, (i % 4 + 1) * rows)

            def step():
                state = (top_out[...], total_out[...], acc_out[...])
                key, value = keys[i // 4][part], values[i // 4][part]
                keep(softmax_step(state, scores_of(stacked, key), value))

            if i:
                pl.when(source < ctx)(step)
            else:
                scores = jnp.where(seen, scores_of(stacked, keys[0][part]), -huge_value)
                keep(softmax_step((none - huge_value, none, none), scores, values[0][part]))

    pl.when(core == 0)(lambda: attend((near, far), (other_near, other_far)))
    pl.when(core == 1)(lambda: attend((other_near, other_far), (near, far)))


def attend_pages(queries, pairs, state_in, done):
    core = lax.axis_index("tp") % 2
    heads, rows, _ = queries.shape
    none = jnp.zeros((heads * rows, HEAD_DIM), jnp.float32)

    def attend(which):
        stacked = queries[...].reshape(heads * rows, HEAD_DIM)
        state = tuple(ref[...] for ref in state_in) or (none - huge_value, none, none)
        for pair in pairs:
            keys, values = pair[which], pair[1 - which]
            state = softmax_step(state, scores_of(stacked, keys[...]), values[...])
        done(state)

    pl.when(core == 0)(lambda: attend(0))
    pl.when(core == 1)(lambda: attend(1))


def pages_kernel(count, queries, *refs):
    pairs = [refs[2 * i : 2 * i + 2] for i in range(count)]
    state_in, state_out = refs[2 * count : -3], refs[-3:]

    def done(state):
        for ref, value in zip(state_out, state):
            ref[...] = value

    attend_pages(queries, pairs, state_in, done)


def last_kernel(
    page_table, page_counts, queries, own, other, top_in, total_in, acc_in,
    turn_top, turn_total, turn_acc, b0, b1, b3, b2, out, cache_out, zero_buf, sems,
):
    ctx = lax.axis_index("ctx")
    heads, rows, _ = queries.shape
    zero_buf[...] = jnp.zeros_like(zero_buf)
    held = b0.shape[0] // (2 * PAGE)
    waits = []
    for r, block in ((0, b0), (1, b1), (3, b3), (2, b2)):
        for half in range(2):
            slot = ctx ^ (r + 4 * half)
            page = page_table[ctx, slot] - slot * held + half * held
            live = page_counts[ctx, slot] > 0
            start = pl.multiple_of(page * PAGE, PAGE)
            place = cache_out.at[pl.ds(pl.multiple_of(slot * PAGE, PAGE), PAGE)]
            sem = sems.at[r, half]

            @pl.when(live)
            def _():
                pltpu.make_async_copy(block.at[pl.ds(start, PAGE)], place, sem).start()

            @pl.when(jnp.logical_not(live))
            def _():
                pltpu.make_async_copy(zero_buf, place, sem).start()

            waits.append(pltpu.make_async_copy(zero_buf, place, sem))

    def done(state):
        top, total, acc = state
        most = jnp.maximum(top, turn_top[...])
        scale = jnp.exp2((top - most) * SCORE_SCALE)
        turn_scale = jnp.exp2((turn_top[...] - most) * SCORE_SCALE)
        total = total * scale + turn_total[...] * turn_scale
        acc = acc * scale + turn_acc[...] * turn_scale
        result = acc / jnp.sum(total, axis=1, keepdims=True)
        result = result.astype(jnp.bfloat16)
        for head in range(heads):
            out[:, head * HEAD_DIM : (head + 1) * HEAD_DIM] = result[head * rows : (head + 1) * rows]

    attend_pages(queries, [(own, other)], (top_in, total_in, acc_in), done)
    for wait in waits:
        wait.wait()


def local(stored_pages, kv_weight, page_table, page_counts, queries, turn_kv, turn_pos):
    ctx_index = lax.axis_index("ctx")
    tp_index = lax.axis_index("tp")
    held, page_rows, width = stored_pages.shape
    rows = held * page_rows
    tok_new = queries.shape[0]
    heads_dev = queries.shape[1] // HEAD_DIM
    bf16 = jnp.bfloat16
    f32 = jnp.float32
    params = pltpu.CompilerParams(vmem_limit_bytes=VMEM_BYTES)

    own_x = stored_pages.reshape(rows, width)
    first, rest = pl.pallas_call(
        pick_kernel,
        out_shape=(
            jax.ShapeDtypeStruct((2 * width, HEAD_DIM), bf16),
            jax.ShapeDtypeStruct((2, 2 * width, HEAD_DIM), bf16),
        ),
        in_specs=[hbm_spec()],
        out_specs=(hbm_spec(),) * 2,
        scratch_shapes=[pltpu.SemaphoreType.DMA((3,))],
        compiler_params=params,
        name="pick",
    )(kv_weight)
    first, rest, turn_kv = lax.optimization_barrier((first, rest, turn_kv))
    first = across(first)
    rest = across(rest)
    local_pos = lax.dynamic_slice_in_dim(turn_pos, ctx_index * tok_new, tok_new)
    within = jnp.arange(rows, dtype=jnp.int32)
    page_pos = [ctx_index * rows + within, (ctx_index ^ 4) * rows + within]
    cosine, sine = rope_tables(jnp.concatenate([local_pos] + page_pos))

    query_heads, turn_block = pl.pallas_call(
        prepare_kernel,
        out_shape=(
            jax.ShapeDtypeStruct((heads_dev, tok_new, HEAD_DIM), bf16),
            jax.ShapeDtypeStruct((tok_new, HEAD_DIM), bf16),
        ),
        in_specs=[vmem_spec()] * 4,
        out_specs=(vmem_spec(), vmem_spec()),
        compiler_params=params,
        name="prepare",
    )(queries, turn_kv, cosine[:tok_new], sine[:tok_new])
    turn_pair = jnp.concatenate([turn_block, shifted(turn_block, 4)])
    carried = shifted(jnp.concatenate([first, turn_pair]), 1)
    relayed = carried[: 2 * width]
    turn_near = jnp.concatenate([turn_pair, carried[2 * width :]])

    x1 = swapped(own_x, 4)
    x3 = swapped(own_x, 12)
    x2a = swapped(x1[: rows // 2], 12)
    x2b = swapped(x3[rows // 2 :], 4)
    late_x, x1 = lax.optimization_barrier((own_x, x1))
    own_pair = swapped(late_x, 1)

    pieces = [own_x, own_pair]
    for piece in (x1, x3, x2a, x2b):
        pieces += [piece, swapped(piece, 1)]

    part_shape = jax.ShapeDtypeStruct((rows, HEAD_DIM), bf16)
    own_part, near_part, far_part = pl.pallas_call(
        project_kernel,
        out_shape=(jax.ShapeDtypeStruct((rows, HEAD_DIM), f32), part_shape, part_shape),
        in_specs=[any_spec()] * 14,
        out_specs=(vmem_spec(),) * 3,
        scratch_shapes=[
            pltpu.VMEM((4, rows, 2 * width), bf16),
            pltpu.VMEM((4, 2 * width, 2 * HEAD_DIM), bf16),
            pltpu.SemaphoreType.DMA((4, 2, 4)),
        ],
        compiler_params=params,
        name="project",
    )(*pieces, kv_weight, first, rest, relayed)
    turn_far = shifted(turn_near, 3)
    got1 = swapped(far_part, 2)
    got2 = shifted(near_part, 4)
    got3 = across(far_part)
    own_block = pl.pallas_call(
        finish_kernel,
        out_shape=jax.ShapeDtypeStruct((2 * rows, HEAD_DIM), bf16),
        in_specs=[vmem_spec()] * 6,
        out_specs=vmem_spec(),
        compiler_params=params,
        name="finish",
    )(own_part, got1, got2, got3, cosine[tok_new:], sine[tok_new:])
    blocks = [own_block] + [shifted(own_block, bits) for bits in (1, 3, 2)]
    own_pair = swapped(own_block, 1)

    def cost(keys):
        work = heads_dev * tok_new * keys
        return pl.CostEstimate(
            flops=4 * work * HEAD_DIM, bytes_accessed=4 * 1024 * 1024, transcendentals=work
        )

    state_shape = (jax.ShapeDtypeStruct((heads_dev * tok_new, HEAD_DIM), f32),) * 3
    turn_state = pl.pallas_call(
        turn_kernel,
        out_shape=state_shape,
        in_specs=[vmem_spec()] * 5,
        out_specs=(vmem_spec(),) * 3,
        compiler_params=params,
        cost_estimate=cost(SOURCES * tok_new),
        name="turn_attention",
    )(query_heads, turn_near, turn_far, swapped(turn_near, 1), swapped(turn_far, 1))

    def attend_more(name, group, state):
        flat = [part for pair in group for part in pair]
        return pl.pallas_call(
            functools.partial(pages_kernel, len(group)),
            out_shape=state_shape,
            in_specs=[vmem_spec()] * (1 + len(flat) + len(state)),
            out_specs=(vmem_spec(),) * 3,
            compiler_params=params,
            cost_estimate=cost(2 * rows * len(group)),
            name=name,
        )(query_heads, *flat, *state)

    state = attend_more("pages_near", [(own_block, own_pair)], ())
    blocks[1], blocks[2], state, turn_state = lax.optimization_barrier(
        (blocks[1], blocks[2], state, turn_state)
    )
    pairs = [(block, swapped(block, 1)) for block in blocks[1:]]
    state = attend_more("pages_side", pairs[:2], state)
    attended, cache = pl.pallas_call(
        last_kernel,
        out_shape=(
            jax.ShapeDtypeStruct((tok_new, heads_dev * HEAD_DIM), bf16),
            jax.ShapeDtypeStruct((SOURCES * PAGE, HEAD_DIM), bf16),
        ),
        in_specs=[smem_spec(), smem_spec()] + [vmem_spec()] * 9 + [any_spec()] * 4,
        out_specs=(vmem_spec(), any_spec()),
        scratch_shapes=[
            pltpu.VMEM((PAGE, HEAD_DIM), bf16),
            pltpu.SemaphoreType.DMA((4, 2)),
        ],
        compiler_params=params,
        cost_estimate=cost(2 * rows),
        name="pages_last",
    )(page_table, page_counts, query_heads, *pairs[2], *state, *turn_state, *blocks)
    return (attended, cache)


def solution(mesh):
    placed = (P("ctx", None, "tp"), P(None, "tp"), P(), P(), P("ctx", "tp"), P("ctx", "tp"), P())
    return jax.shard_map(
        local,
        mesh=mesh,
        in_specs=placed,
        out_specs=(P("ctx", "tp"), P("ctx", "tp")),
        check_vma=False,
    )
```

```python
import functools
import math

import jax
import jax.numpy as jnp
from jax import lax
from jax.experimental import pallas as pl
from jax.experimental.pallas import tpu as pltpu
from jax.sharding import PartitionSpec as P

HEAD_DIM = 128
PAGE = 128
SOURCES = 8
huge_value = 1e30
SCORE_SCALE = math.log2(math.e) / math.sqrt(HEAD_DIM)
VMEM_BYTES = 32 * 1024 * 1024


def swapped(value, bits):
    return lax.ppermute(value, "tp", [(i, i ^ bits) for i in range(lax.axis_size("tp"))])


def shifted(value, bits):
    return lax.ppermute(value, "ctx", [(i, i ^ bits) for i in range(lax.axis_size("ctx"))])


def across(value):
    peers = lax.axis_size("ctx") * lax.axis_size("tp")
    flip = 4 * lax.axis_size("tp") + 2
    return lax.ppermute(value, ("ctx", "tp"), [(i, i ^ flip) for i in range(peers)])


def inverse_freq(head_width):
    half_width = head_width // 2
    exponent = jnp.arange(half_width, dtype=jnp.float32) * 2.0 / head_width
    base_freq = jnp.exp(-exponent * math.log(500000.0))
    wavelength = 2.0 * math.pi / base_freq
    smooth = (8192.0 / wavelength - 1.0) / 3.0
    blended = (1.0 - smooth) * base_freq / 8.0 + smooth * base_freq
    return jnp.where(
        wavelength < 2048.0, base_freq, jnp.where(wavelength > 8192.0, base_freq / 8.0, blended)
    )


def rope_tables(positions):
    angle = positions.astype(jnp.float32)[:, None] * inverse_freq(HEAD_DIM)[None, :]
    cosine = jnp.cos(angle)
    sine = jnp.sin(angle)
    return (
        jnp.concatenate([cosine, cosine], axis=1),
        jnp.concatenate([-sine, sine], axis=1),
    )


def turned(value, cosine, sine):
    return value * cosine + pltpu.roll(value, HEAD_DIM // 2, 1) * sine


def any_spec():
    return pl.BlockSpec(memory_space=pl.ANY)


def hbm_spec():
    return pl.BlockSpec(memory_space=pltpu.HBM)


def vmem_spec():
    return pl.BlockSpec(memory_space=pltpu.VMEM)


def smem_spec():
    return pl.BlockSpec(memory_space=pltpu.SMEM)


def prepare_kernel(queries, turn_kv, cosine, sine, query_out, turn_out):
    is_key = lax.axis_index("tp") % 2 == 0
    c = cosine[...]
    s = sine[...]
    for head in range(query_out.shape[0]):
        block = queries[:, head * HEAD_DIM : (head + 1) * HEAD_DIM].astype(jnp.float32)
        query_out[head] = turned(block, c, s).astype(jnp.bfloat16)
    block = turn_kv[...].astype(jnp.float32)
    block = turned(block, jnp.where(is_key, c, 1.0), jnp.where(is_key, s, 0.0)).astype(jnp.bfloat16)
    turn_out[...] = block


def pick_kernel(weight, first_out, rest_out, sems):
    odd = lax.axis_index("ctx") % 2
    far = 1 - (lax.axis_index("tp") // 2) % 2
    depth = first_out.shape[0]
    copies = []
    for i, (group, out) in enumerate(((3 * odd, first_out), (1, rest_out.at[0]), (2, rest_out.at[1]))):
        row = pl.multiple_of((group * 2 + far) * depth, depth)
        copies.append(pltpu.make_async_copy(weight.at[pl.ds(row, depth)], out, sems.at[i]))
    for copy in copies:
        copy.start()
    for copy in copies:
        copy.wait()


def project_kernel(*refs):
    slices = refs[:10]
    weight, first, rest, relayed, own_out, near_out, far_out, x_buf, w_buf, sems = refs[10:]
    odd = lax.axis_index("ctx") % 2
    tp = lax.axis_index("tp")
    low = tp % 4
    spot = tp // 4
    rows = x_buf.shape[1]
    depth = slices[0].shape[1]

    def far_copy(at, r, half, act):
        part = pl.ds(half * depth, depth)
        source = pl.ds(pl.multiple_of(((low % 2) ^ half) * depth, depth), depth)

        def go(ref):
            place = w_buf.at[r, part, pl.ds(HEAD_DIM, HEAD_DIM)]
            act(pltpu.make_async_copy(ref.at[source], place, sems.at[r, half, 1]))

        pl.when(at == 3 * odd)(lambda: go(first))
        pl.when(at == 1)(lambda: go(rest.at[0]))
        pl.when(at == 2)(lambda: go(rest.at[1]))
        pl.when(at == 3 - 3 * odd)(lambda: go(relayed))

    copies = []
    for i, r in enumerate((0, 1, 3, 2)):
        at = spot ^ r
        for half in range(2):
            part = pl.ds(half * depth, depth)
            near_row = pl.multiple_of((at * 4 + (low ^ half)) * depth, depth)
            group = [
                pltpu.make_async_copy(
                    weight.at[pl.ds(near_row, depth)],
                    w_buf.at[r, part, pl.ds(0, HEAD_DIM)],
                    sems.at[r, half, 0],
                ),
            ]
            sent = [(slices[2 * i + half], 0, rows)]
            if r == 2:
                sent = [(slices[6 + half], 0, rows // 2), (slices[8 + half], rows // 2, rows // 2)]
            for k, (piece, start, count) in enumerate(sent):
                place = x_buf.at[r, pl.ds(start, count), part]
                group.append(pltpu.make_async_copy(piece, place, sems.at[r, half, 2 + k]))
            for copy in group:
                copy.start()
            far_copy(at, r, half, lambda copy: copy.start())
            copies.append(group)
    total = None
    for i, r in enumerate((0, 1, 3, 2)):
        for half in range(2):
            for copy in copies[2 * i + half]:
                copy.wait()
            far_copy(spot ^ r, r, half, lambda copy: copy.wait())
        part = jnp.dot(x_buf[r], w_buf[r], preferred_element_type=jnp.float32)
        total = part if total is None else total + part
    own_out[...] = total[:, :HEAD_DIM]
    near_out[...] = total[:, :HEAD_DIM].astype(jnp.bfloat16)
    far_out[...] = total[:, HEAD_DIM:].astype(jnp.bfloat16)


def finish_kernel(own, p1, p2, p3, cosine, sine, out):
    is_key = lax.axis_index("tp") % 2 == 0
    rows = own.shape[0]
    mine = own[...] + p1[...].astype(jnp.float32)
    other = p2[...].astype(jnp.float32) + p3[...].astype(jnp.float32)
    for i, value in enumerate((mine, other)):
        c = jnp.where(is_key, cosine[i * rows : (i + 1) * rows], 1.0)
        s = jnp.where(is_key, sine[i * rows : (i + 1) * rows], 0.0)
        out[i * rows : (i + 1) * rows] = turned(value, c, s).astype(jnp.bfloat16)


def scores_of(query, keys):
    return lax.dot_general(
        query, keys, (((1,), (1,)), ((), ())), preferred_element_type=jnp.float32
    )


def widened(value, width):
    return value if width == HEAD_DIM else jnp.concatenate([value] * (width // HEAD_DIM), axis=1)


def softmax_step(state, scores, values):
    top, total, acc = state
    width = scores.shape[1]
    new_top = jnp.maximum(top, jnp.max(scores, axis=1, keepdims=True))
    decay = jnp.exp2((top - new_top) * SCORE_SCALE)
    weights = jnp.exp2((scores - widened(new_top, width)) * SCORE_SCALE)
    total = total * decay
    for at in range(0, width, HEAD_DIM):
        total = total + weights[:, at : at + HEAD_DIM]
    acc = acc * decay + jnp.dot(
        weights.astype(jnp.bfloat16), values, preferred_element_type=jnp.float32
    )
    return new_top, total, acc


def turn_kernel(queries, near, far, other_near, other_far, top_out, total_out, acc_out):
    ctx = lax.axis_index("ctx")
    core = lax.axis_index("tp") % 2
    heads, rows, _ = queries.shape
    stacked = queries[...].reshape(heads * rows, HEAD_DIM)
    shape = (heads * rows, rows)
    token = lax.broadcasted_iota(jnp.int32, shape, 0) % rows
    seen = lax.broadcasted_iota(jnp.int32, shape, 1) <= token

    def keep(state):
        top_out[...], total_out[...], acc_out[...] = state

    none = jnp.zeros(top_out.shape, jnp.float32)

    def attend(keys, values):
        for i in range(SOURCES):
            source = ctx ^ ((0, 4, 1, 5, 3, 7, 2, 6)[i])
            part = slice(i % 4 * rows, (i % 4 + 1) * rows)

            def step():
                state = (top_out[...], total_out[...], acc_out[...])
                key, value = keys[i // 4][part], values[i // 4][part]
                keep(softmax_step(state, scores_of(stacked, key), value))

            if i:
                pl.when(source < ctx)(step)
            else:
                scores = jnp.where(seen, scores_of(stacked, keys[0][part]), -huge_value)
                keep(softmax_step((none - huge_value, none, none), scores, values[0][part]))

    pl.when(core == 0)(lambda: attend((near, far), (other_near, other_far)))
    pl.when(core == 1)(lambda: attend((other_near, other_far), (near, far)))


def attend_pages(queries, pairs, state_in, done):
    core = lax.axis_index("tp") % 2
    heads, rows, _ = queries.shape
    none = jnp.zeros((heads * rows, HEAD_DIM), jnp.float32)

    def attend(which):
        stacked = queries[...].reshape(heads * rows, HEAD_DIM)
        state = tuple(ref[...] for ref in state_in) or (none - huge_value, none, none)
        for pair in pairs:
            keys, values = pair[which], pair[1 - which]
            state = softmax_step(state, scores_of(stacked, keys[...]), values[...])
        done(state)

    pl.when(core == 0)(lambda: attend(0))
    pl.when(core == 1)(lambda: attend(1))


def merged(state, others):
    top, total, acc = state
    most = jnp.maximum(top, others[0][...])
    scale = jnp.exp2((top - most) * SCORE_SCALE)
    other_scale = jnp.exp2((others[0][...] - most) * SCORE_SCALE)
    total = total * scale + others[1][...] * other_scale
    return most, total, acc * scale + others[2][...] * other_scale


def pages_kernel(count, queries, *refs):
    pairs = [refs[2 * i : 2 * i + 2] for i in range(count)]
    state_in, others, state_out = refs[2 * count : -3][:3], refs[2 * count : -3][3:], refs[-3:]

    def done(state):
        if others:
            state = merged(state, others)
        for ref, value in zip(state_out, state):
            ref[...] = value

    attend_pages(queries, pairs, state_in, done)


def last_kernel(
    page_table, page_counts, queries, own, other, top_in, total_in, acc_in, b0, b1, b3, b2,
    out, cache_out, zero_buf, sems,
):
    ctx = lax.axis_index("ctx")
    heads, rows, _ = queries.shape
    zero_buf[...] = jnp.zeros_like(zero_buf)
    held = b0.shape[0] // (2 * PAGE)
    waits = []
    for r, block in ((0, b0), (1, b1), (3, b3), (2, b2)):
        for half in range(2):
            slot = ctx ^ (r + 4 * half)
            page = page_table[ctx, slot] - slot * held + half * held
            live = page_counts[ctx, slot] > 0
            start = pl.multiple_of(page * PAGE, PAGE)
            place = cache_out.at[pl.ds(pl.multiple_of(slot * PAGE, PAGE), PAGE)]
            sem = sems.at[r, half]

            @pl.when(live)
            def _():
                pltpu.make_async_copy(block.at[pl.ds(start, PAGE)], place, sem).start()

            @pl.when(jnp.logical_not(live))
            def _():
                pltpu.make_async_copy(zero_buf, place, sem).start()

            waits.append(pltpu.make_async_copy(zero_buf, place, sem))

    def done(state):
        result = state[2] * (1.0 / jnp.sum(state[1], axis=1, keepdims=True))
        result = result.astype(jnp.bfloat16)
        for head in range(heads):
            out[:, head * HEAD_DIM : (head + 1) * HEAD_DIM] = result[head * rows : (head + 1) * rows]

    attend_pages(queries, [(own, other)], (top_in, total_in, acc_in), done)
    for wait in waits:
        wait.wait()


def local(stored_pages, kv_weight, page_table, page_counts, queries, turn_kv, turn_pos):
    ctx_index = lax.axis_index("ctx")
    tp_index = lax.axis_index("tp")
    held, page_rows, width = stored_pages.shape
    rows = held * page_rows
    tok_new = queries.shape[0]
    heads_dev = queries.shape[1] // HEAD_DIM
    bf16 = jnp.bfloat16
    f32 = jnp.float32
    params = pltpu.CompilerParams(vmem_limit_bytes=VMEM_BYTES)

    own_x = stored_pages.reshape(rows, width)
    first, rest = pl.pallas_call(
        pick_kernel,
        out_shape=(
            jax.ShapeDtypeStruct((2 * width, HEAD_DIM), bf16),
            jax.ShapeDtypeStruct((2, 2 * width, HEAD_DIM), bf16),
        ),
        in_specs=[hbm_spec()],
        out_specs=(hbm_spec(),) * 2,
        scratch_shapes=[pltpu.SemaphoreType.DMA((3,))],
        compiler_params=params,
        name="pick",
    )(kv_weight)
    first, rest, turn_kv = lax.optimization_barrier((first, rest, turn_kv))
    first = across(first)
    rest = across(rest)
    local_pos = lax.dynamic_slice_in_dim(turn_pos, ctx_index * tok_new, tok_new)
    within = jnp.arange(rows, dtype=jnp.int32)
    page_pos = [ctx_index * rows + within, (ctx_index ^ 4) * rows + within]
    cosine, sine = rope_tables(jnp.concatenate([local_pos] + page_pos))

    query_heads, turn_block = pl.pallas_call(
        prepare_kernel,
        out_shape=(
            jax.ShapeDtypeStruct((heads_dev, tok_new, HEAD_DIM), bf16),
            jax.ShapeDtypeStruct((tok_new, HEAD_DIM), bf16),
        ),
        in_specs=[vmem_spec()] * 4,
        out_specs=(vmem_spec(), vmem_spec()),
        compiler_params=params,
        name="prepare",
    )(queries, turn_kv, cosine[:tok_new], sine[:tok_new])
    turn_pair = jnp.concatenate([turn_block, shifted(turn_block, 4)])
    relayed = shifted(first, 1)
    turn_near = jnp.concatenate([turn_pair, shifted(turn_pair, 1)])

    x1 = swapped(own_x, 4)
    x3 = swapped(own_x, 12)
    x2a = swapped(x1[: rows // 2], 12)
    x2b = swapped(x3[rows // 2 :], 4)
    late_x, x1 = lax.optimization_barrier((own_x, x1))
    own_pair = swapped(late_x, 1)

    pieces = [own_x, own_pair]
    for piece in (x1, x3, x2a, x2b):
        pieces += [piece, swapped(piece, 1)]

    part_shape = jax.ShapeDtypeStruct((rows, HEAD_DIM), bf16)
    own_part, near_part, far_part = pl.pallas_call(
        project_kernel,
        out_shape=(jax.ShapeDtypeStruct((rows, HEAD_DIM), f32), part_shape, part_shape),
        in_specs=[any_spec()] * 14,
        out_specs=(vmem_spec(),) * 3,
        scratch_shapes=[
            pltpu.VMEM((4, rows, 2 * width), bf16),
            pltpu.VMEM((4, 2 * width, 2 * HEAD_DIM), bf16),
            pltpu.SemaphoreType.DMA((4, 2, 4)),
        ],
        compiler_params=params,
        name="project",
    )(*pieces, kv_weight, first, rest, relayed)
    turn_near, far_part = lax.optimization_barrier((turn_near, far_part))
    turn_far = shifted(turn_near, 3)
    got1 = swapped(far_part, 2)
    got2 = shifted(near_part, 4)
    got3 = across(far_part)
    own_block = pl.pallas_call(
        finish_kernel,
        out_shape=jax.ShapeDtypeStruct((2 * rows, HEAD_DIM), bf16),
        in_specs=[vmem_spec()] * 6,
        out_specs=vmem_spec(),
        compiler_params=params,
        name="finish",
    )(own_part, got1, got2, got3, cosine[tok_new:], sine[tok_new:])
    blocks = [own_block] + [shifted(own_block, bits) for bits in (1, 3, 2)]
    own_pair = swapped(own_block, 1)

    def cost(keys):
        work = heads_dev * tok_new * keys
        return pl.CostEstimate(
            flops=4 * work * HEAD_DIM, bytes_accessed=4 * 1024 * 1024, transcendentals=work
        )

    state_shape = (jax.ShapeDtypeStruct((heads_dev * tok_new, HEAD_DIM), f32),) * 3
    turn_state = pl.pallas_call(
        turn_kernel,
        out_shape=state_shape,
        in_specs=[vmem_spec()] * 5,
        out_specs=(vmem_spec(),) * 3,
        compiler_params=params,
        cost_estimate=cost(SOURCES * tok_new),
        name="turn_attention",
    )(query_heads, turn_near, turn_far, swapped(turn_near, 1), swapped(turn_far, 1))

    def attend_more(name, group, state):
        flat = [part for pair in group for part in pair]
        return pl.pallas_call(
            functools.partial(pages_kernel, len(group)),
            out_shape=state_shape,
            in_specs=[vmem_spec()] * (1 + len(flat) + len(state)),
            out_specs=(vmem_spec(),) * 3,
            compiler_params=params,
            cost_estimate=cost(2 * rows * len(group)),
            name=name,
        )(query_heads, *flat, *state)

    state = attend_more("pages_near", [(own_block, own_pair)], ())
    blocks[1], blocks[2], state, turn_state = lax.optimization_barrier(
        (blocks[1], blocks[2], state, turn_state)
    )
    pairs = [(block, swapped(block, 1)) for block in blocks[1:3]]
    state = attend_more("pages_side", pairs, (*state, *turn_state))
    attended, cache = pl.pallas_call(
        last_kernel,
        out_shape=(
            jax.ShapeDtypeStruct((tok_new, heads_dev * HEAD_DIM), bf16),
            jax.ShapeDtypeStruct((SOURCES * PAGE, HEAD_DIM), bf16),
        ),
        in_specs=[smem_spec(), smem_spec()] + [vmem_spec()] * 6 + [any_spec()] * 4,
        out_specs=(vmem_spec(), any_spec()),
        scratch_shapes=[
            pltpu.VMEM((PAGE, HEAD_DIM), bf16),
            pltpu.SemaphoreType.DMA((4, 2)),
        ],
        compiler_params=params,
        cost_estimate=cost(2 * rows),
        name="pages_last",
    )(page_table, page_counts, query_heads, blocks[3], swapped(blocks[3], 1), *state, *blocks)
    return (attended, cache)


def solution(mesh):
    placed = (P("ctx", None, "tp"), P(None, "tp"), P(), P(), P("ctx", "tp"), P("ctx", "tp"), P())
    return jax.shard_map(
        local,
        mesh=mesh,
        in_specs=placed,
        out_specs=(P("ctx", "tp"), P("ctx", "tp")),
        check_vma=False,
    )
```
